128 devices in a mesh: rows: 32 (over x, z_hi, y), ch: 4 (over z_lo, core).
Axes of the slice: x: 4, y: 4, z: 4 (z_hi: 2, z_lo: 2; z = z_hi * 2 + z_lo), core: 2. Of those that a mesh axis runs over, the one named last changes fastest.
Arguments:
- pair: bfloat16 [128, 512, 512], P('ch', 'rows'), may hold values from -6 to 6
- residue_mask: int32 [512], replicated, may hold values 0 or 1
- chain_ids: int32 [512], replicated, may hold values from 0 to 3, never falling along the last dimension, each value on 1 to 256 neighbouring positions
- pair_gain: float32 [2, 128], replicated, may hold values from 0.1 to 1.9
- pair_bias: float32 [2, 128], replicated, may hold values from -3 to 3
- in_weight: bfloat16 [2, 4, 128, 128], P(None, None, None, 'ch'), may hold values from -0.5 to 0.5
- gate_weight: bfloat16 [2, 128, 128], P(None, None, 'ch'), may hold values from -0.5 to 0.5
- hidden_gain: float32 [2, 128], P(None, 'ch'), may hold values from 0.1 to 1.9
- hidden_bias: float32 [2, 128], P(None, 'ch'), may hold values from -3 to 3
- cross_gain: float32 [2, 128], P(None, 'ch'), may hold values from 0.3 to 1.7
- out_weight: bfloat16 [2, 128, 128], replicated, may hold values from -0.5 to 0.5
Outputs:
- pair_out: bfloat16 [128, 512, 512], P('ch', 'rows')
The draws below stay inside these ranges and needn't reach their ends.
Inputs may be any that keep to these rules, and one draw needn't show every extreme that they name: `chain_ids`: chain numbers never fall along the residues; every chain has 1 to N // 2 residues and one has exactly N // 2.
All inputs are finite; a program needn't handle non-finite values.
Results may differ from the reference program's by a relative error of at most 0.014.
Values may be sent and summed in bfloat16 or wider, within the bound.
A program may use at most 192 MiB of HBM per device.

```python
import math
import jax
import jax.numpy as jnp
import numpy as np
from jax import lax

C = 128
HID = 128
N = 512


def place_ends(drawn, stream_key, least, high):
    spot = [jax.random.randint(jax.random.fold_in(stream_key, axis), (), 0, length) for axis, length in enumerate(drawn.shape)]
    longest = drawn.shape.index(max(drawn.shape))
    neighbour = spot[:longest] + [(spot[longest] + 1) % drawn.shape[longest]] + spot[longest + 1:]
    return drawn.at[tuple(spot)].set(least).at[tuple(neighbour)].set(high)


def level_of(rng, shape, cuts, low, largest):
    factor_of, own = 1.0, jax.random.fold_in(rng, 6)
    for axis_at, parts in cuts:
        heights = jnp.exp(jax.random.uniform(jax.random.fold_in(own, axis_at), (parts,), jnp.float32, low / len(cuts), largest / len(cuts)))
        factor_of = factor_of * jnp.repeat(heights, shape[axis_at] // parts).reshape([-1 if axis == axis_at else 1 for axis in range(len(shape))])
    return factor_of


def split_up(amount, total, reach, skew):
    loads = [(1 << 20) // math.isqrt(grade ** skew) + 1 for grade in range(2, amount + 1)]
    surplus, holding = total - reach - (amount - 1), [1] * (amount - 1)
    while surplus > 0:
        free = [i for i in range(amount - 1) if holding[i] < reach]
        whole, left = sum([loads[i] for i in free]), surplus
        for i in free:
            addition = min(reach - holding[i], max(1, left * loads[i] // whole), surplus)
            holding[i] = holding[i] + addition
            surplus = surplus - addition
    return np.array([reach] + holding)


def ragged_sizes(stream_key, count, total, most, skew):
    if count == 2:
        one = jax.random.randint(stream_key, (), max(1, total - most), min(most, total - 1) + 1)
        return jnp.stack([one, total - one])
    lengths = jnp.asarray(split_up(count, total, most, skew), jnp.int32)
    couples = (count - 1) // 2
    source_of, sink = lengths[1:1 + 2 * couples:2], lengths[2:2 + 2 * couples:2]
    margin = jnp.minimum(source_of - 1, most - sink)
    passed = jax.random.randint(jax.random.fold_in(stream_key, 1), (couples,), 0, 1 << 20) % (margin + 1)
    lengths = lengths.at[1:1 + 2 * couples:2].set(source_of - passed).at[2:2 + 2 * couples:2].set(sink + passed)
    return lengths[jax.random.permutation(jax.random.fold_in(stream_key, 2), count)]


def normal_values(key, extent, scale, reach, split=(), held_as=jnp.bfloat16):
    entries = scale * jax.random.normal(key, extent, jnp.float32)
    if split:
        entries = entries * level_of(key, extent, split, -0.22, 0.18)
    return jnp.clip(entries, -reach, reach).astype(held_as)


def setup_inputs(seed: int = 0) -> dict:
    key_list = jax.random.split(jax.random.key(seed), 12)
    pair = normal_values(key_list[0], (C, N, N), 1.0, 6.0, ((0, 4), (1, 32)))
    residue_mask = place_ends((jax.random.randint(key_list[1], (N,), 0, 8) < 7).astype(jnp.int32), jax.random.fold_in(key_list[1], 1), 0, 1)
    chain_ids = jnp.searchsorted(jnp.cumsum(ragged_sizes(key_list[2], 4, N, N // 2, 0)), jnp.arange(N), side="right").astype(jnp.int32)
    pair_gain = jnp.clip(1.0 + 0.18 * jax.random.normal(key_list[3], (2, C), jnp.float32), 0.1, 1.9)
    pair_bias = normal_values(key_list[4], (2, C), 0.5, 3.0, (), jnp.float32)
    in_weight = normal_values(key_list[5], (2, 4, C, HID), C ** -0.5, 0.5, ((3, 4),))
    gate_weight = normal_values(key_list[6], (2, C, C), C ** -0.5, 0.5, ((2, 4),))
    hidden_gain = jnp.clip(1.0 + 0.18 * jax.random.normal(key_list[7], (2, HID), jnp.float32), 0.1, 1.9)
    hidden_bias = normal_values(key_list[8], (2, HID), 0.5, 3.0, ((1, 4),), jnp.float32)
    cross_gain = jnp.clip(0.3 + 1.40000004 * jax.random.uniform(key_list[9], (2, HID), jnp.float32) ** level_of(key_list[9], (2, HID), ((1, 4),), -0.2, 0.2), 0.3, 1.7)
    out_weight = normal_values(key_list[10], (2, HID, C), HID ** -0.5, 0.5)
    return dict(pair=pair, residue_mask=residue_mask, chain_ids=chain_ids, pair_gain=pair_gain, pair_bias=pair_bias, in_weight=in_weight, gate_weight=gate_weight, hidden_gain=hidden_gain, hidden_bias=hidden_bias, cross_gain=cross_gain, out_weight=out_weight)


def layer_norm(values, gain, offset):
    center = lax.optimization_barrier(jnp.mean(values, axis=0))
    spread = lax.optimization_barrier(jnp.mean(values * values, axis=0)) - center * center
    return (values - center) * lax.rsqrt(spread + 1e-05) * gain[:, None, None] + offset[:, None, None]

def reference(pair, residue_mask, chain_ids, pair_gain, pair_bias, in_weight, gate_weight, hidden_gain, hidden_bias, cross_gain, out_weight):
    maskf = residue_mask.astype(jnp.float32)
    pair_mask = maskf[:, None] * maskf[None, :]
    crossing = chain_ids[:, None] != chain_ids[None, :]
    current = pair
    for layer in range(2):
        pair_f = current.astype(jnp.float32)
        normed = layer_norm(pair_f, pair_gain[layer], pair_bias[layer]).astype(jnp.bfloat16)
        normed_f = normed.astype(jnp.float32)
        proj = jnp.einsum('pch,cij->phij', in_weight[layer].astype(jnp.float32), normed_f)
        factor = pair_mask[None] * jnp.where(crossing[None], cross_gain[layer][:, None, None], 1.0)
        left = (factor * jax.nn.sigmoid(proj[0]) * proj[1]).astype(jnp.bfloat16).astype(jnp.float32)
        right = (factor * jax.nn.sigmoid(proj[2]) * proj[3]).astype(jnp.bfloat16).astype(jnp.float32)
        if layer == 0:
            tri = jnp.einsum('hik,hjk->hij', left, right)
        else:
            tri = jnp.einsum('hki,hkj->hij', left, right)
        tri_normed = layer_norm(tri, hidden_gain[layer], hidden_bias[layer]).astype(jnp.bfloat16)
        gate = jax.nn.sigmoid(jnp.einsum('cd,cij->dij', gate_weight[layer].astype(jnp.float32), normed_f))
        update = jnp.einsum('hd,hij->dij', out_weight[layer].astype(jnp.float32), tri_normed.astype(jnp.float32))
        current = (pair_f + gate * update).astype(jnp.bfloat16)
    return current
```

```python
import functools

import jax
import jax.numpy as jnp
from jax import lax
from jax.experimental import pallas as pl
from jax.experimental.pallas import tpu as pltpu
from jax.sharding import PartitionSpec as P

C = 128
HID = 128
N = 512
MESH = pl.DeviceIdType.MESH
VM = pl.BlockSpec(memory_space=pltpu.VMEM)
LIMIT = 48 * 2**20


def greet(partners):
    barrier = pltpu.get_barrier_semaphore()
    for dev in partners:
        pl.semaphore_signal(barrier, inc=1, device_id=dev, device_id_type=MESH)
    pl.semaphore_wait(barrier, len(partners))


def gather_kernel(pair, win, wgate, small, pair_all, win_all, wgate_all, small_all, send, recv, local):
    r = lax.axis_index("rows")
    c = lax.axis_index("ch")
    greet([(r, lax.rem(c + s, 4)) for s in (1, 2, 3)])

    def moves(dst):
        return [
            (pair.at[:, :, pl.ds(pl.multiple_of(dst * 128, 128), 128)], pair_all.at[pl.ds(c * 32, 32)]),
            (win, win_all.at[:, pl.ds(pl.multiple_of(c * 32, 32), 32)]),
            (wgate, wgate_all.at[:, pl.ds(pl.multiple_of(c * 32, 32), 32)]),
            (small, small_all.at[c]),
        ]

    copies = []
    for s in (1, 2, 3):
        dst = lax.rem(c + s, 4)
        for k, (a, b) in enumerate(moves(dst)):
            cp = pltpu.make_async_remote_copy(
                src_ref=a, dst_ref=b, send_sem=send.at[s - 1, k], recv_sem=recv.at[s - 1, k],
                device_id=(r, dst), device_id_type=MESH,
            )
            cp.start()
            copies.append(cp)
    own = [pltpu.make_async_copy(a, b, local.at[k]) for k, (a, b) in enumerate(moves(c))]
    for cp in own:
        cp.start()
    for cp in own + copies:
        cp.wait()


def scatter_kernel(cur, out, send, recv, local):
    r = lax.axis_index("rows")
    c = lax.axis_index("ch")
    greet([(r, lax.rem(c + s, 4)) for s in (1, 2, 3)])
    here = out.at[:, :, pl.ds(pl.multiple_of(c * 128, 128), 128)]
    copies = []
    for s in (1, 2, 3):
        dst = lax.rem(c + s, 4)
        cp = pltpu.make_async_remote_copy(
            src_ref=cur.at[pl.ds(dst * 32, 32)], dst_ref=here, send_sem=send.at[s - 1], recv_sem=recv.at[s - 1],
            device_id=(r, dst), device_id_type=MESH,
        )
        cp.start()
        copies.append(cp)
    own = pltpu.make_async_copy(cur.at[pl.ds(c * 32, 32)], here, local)
    own.start()
    own.wait()
    for cp in copies:
        cp.wait()


def swap_kernel(x, y, send, recv, local):
    me = lax.axis_index("rows") * 4 + lax.axis_index("ch")
    barrier = pltpu.get_barrier_semaphore()

    def place(s):
        d = lax.rem(me + s, 128)
        return d, (lax.div(d, 4), lax.rem(d, 4))

    @pl.loop(1, 128)
    def _(s):
        pl.semaphore_signal(barrier, inc=1, device_id=place(s)[1], device_id_type=MESH)

    pl.semaphore_wait(barrier, 127)

    @pl.loop(1, 128)
    def _(s):
        d, dev = place(s)
        pltpu.make_async_remote_copy(
            src_ref=x.at[d], dst_ref=y.at[me], send_sem=send, recv_sem=recv, device_id=dev, device_id_type=MESH
        ).start()

    own = pltpu.make_async_copy(x.at[me], y.at[me], local)
    own.start()
    own.wait()
    whole = pltpu.make_async_remote_copy(
        src_ref=x.at[pl.ds(0, 127)], dst_ref=y.at[pl.ds(0, 127)], send_sem=send, recv_sem=recv,
        device_id=place(1)[1], device_id_type=MESH,
    )
    whole.wait_recv()
    whole.wait_send()


def gather(*args):
    dma = pltpu.SemaphoreType.DMA
    shape = jax.ShapeDtypeStruct
    return pl.pallas_call(
        gather_kernel,
        out_shape=(
            shape((C, 16, 128), jnp.bfloat16), shape((8, 128, 128), jnp.bfloat16),
            shape((2, 128, 128), jnp.bfloat16), shape((4, 8, 128), jnp.float32),
        ),
        in_specs=[VM] * 4, out_specs=(VM,) * 4,
        scratch_shapes=[dma((3, 4)), dma((3, 4)), dma((4,))],
        compiler_params=pltpu.CompilerParams(collective_id=0, has_side_effects=True, vmem_limit_bytes=LIMIT),
    )(*args)


def scatter(cur):
    dma = pltpu.SemaphoreType.DMA
    return pl.pallas_call(
        scatter_kernel,
        out_shape=jax.ShapeDtypeStruct((32, 16, 512), jnp.bfloat16),
        in_specs=[VM], out_specs=VM,
        scratch_shapes=[dma((3,)), dma((3,)), dma],
        compiler_params=pltpu.CompilerParams(collective_id=3, has_side_effects=True, vmem_limit_bytes=LIMIT),
    )(cur)


def swap(x, cid):
    dma = pltpu.SemaphoreType.DMA
    return pl.pallas_call(
        swap_kernel,
        out_shape=jax.ShapeDtypeStruct(x.shape, x.dtype),
        in_specs=[VM], out_specs=VM,
        scratch_shapes=[dma, dma, dma],
        compiler_params=pltpu.CompilerParams(collective_id=cid, has_side_effects=True, vmem_limit_bytes=LIMIT),
    )(x)


def norm(values, gain, offset):
    center = jnp.mean(values, axis=0)
    spread = jnp.mean(values * values, axis=0) - center * center
    return (
        (values - center) * lax.rsqrt(spread + 1e-05) * gain[:, None, None] + offset[:, None, None]
    ).astype(jnp.bfloat16)


def per_device(
    pair, residue_mask, chain_ids, pair_gain, pair_bias, in_weight, gate_weight,
    hidden_gain, hidden_bias, cross_gain, out_weight,
):
    r = lax.axis_index("rows")
    c = lax.axis_index("ch")
    small = jnp.concatenate([hidden_gain, hidden_bias, cross_gain, jnp.zeros_like(cross_gain)], 0)
    small = jnp.pad(small, ((0, 0), (0, 96)))
    cur, win, wgate, small_all = gather(
        pair, jnp.swapaxes(in_weight, 2, 3).reshape(8, 32, 128), jnp.swapaxes(gate_weight, 1, 2), small
    )
    small_all = jnp.swapaxes(small_all[:, :, :32], 0, 1).reshape(8, 128)
    mask = residue_mask.astype(jnp.float32)
    rows = lambda a: lax.dynamic_slice_in_dim(a, r * 16, 16)
    cols = lambda a: lax.dynamic_slice_in_dim(a, c * 128, 128)
    pair_mask = rows(mask)[:, None] * cols(mask)[None, :]
    crossing = rows(chain_ids)[:, None] != cols(chain_ids)[None, :]
    for u in range(2):
        pair_f = cur.astype(jnp.float32)
        normed = norm(pair_f, pair_gain[u], pair_bias[u])
        proj = jnp.einsum("phc,cij->phij", win[4 * u : 4 * u + 4], normed, preferred_element_type=jnp.float32)
        factor = pair_mask[None] * jnp.where(crossing[None], small_all[4 + u][:, None, None], 1.0)
        left = (factor * jax.nn.sigmoid(proj[0]) * proj[1]).astype(jnp.bfloat16)
        right = (factor * jax.nn.sigmoid(proj[2]) * proj[3]).astype(jnp.bfloat16)
        both = swap(jnp.concatenate([left, right], 1), 1)
        both = both.reshape(32, 4, 2, 16, 128).transpose(2, 0, 3, 1, 4).reshape(2, 512, 512)
        tri = jnp.einsum(
            "ik,jk->ij" if u == 0 else "ki,kj->ij", both[0], both[1], preferred_element_type=jnp.float32
        ).astype(jnp.bfloat16)
        tri = swap(tri.reshape(32, 16, 4, 128).transpose(0, 2, 1, 3).reshape(128, 16, 128), 2)
        tri_normed = norm(tri.astype(jnp.float32), small_all[u], small_all[2 + u])
        gate = jax.nn.sigmoid(jnp.einsum("dc,cij->dij", wgate[u], normed, preferred_element_type=jnp.float32))
        update = jnp.einsum("hd,hij->dij", out_weight[u], tri_normed, preferred_element_type=jnp.float32)
        cur = (pair_f + gate * update).astype(jnp.bfloat16)
    return scatter(cur)


def solution(mesh):
    placed = (
        P("ch", "rows", None), P(), P(), P(), P(), P(None, None, None, "ch"), P(None, None, "ch"),
        P(None, "ch"), P(None, "ch"), P(None, "ch"), P(),
    )
    return jax.shard_map(
        per_device, mesh=mesh, in_specs=placed, out_specs=P("ch", "rows", None), check_vma=False
    )
```

```python
import jax
import jax.numpy as jnp
from jax import lax
from jax.experimental import pallas as pl
from jax.experimental.pallas import tpu as pltpu
from jax.sharding import PartitionSpec as P

MESH = pl.DeviceIdType.MESH
VM = pl.BlockSpec(memory_space=pltpu.VMEM)
ANY = pl.BlockSpec(memory_space=pl.ANY)
F32 = jnp.float32
BF16 = jnp.bfloat16


def aligned(index, size):
    return pl.ds(pl.multiple_of(index * size, size), size)


def sigmoid(v):
    return 0.5 * jnp.tanh(0.5 * v) + 0.5


def norm(v, gain, offset):
    center = jnp.mean(v, axis=0, keepdims=True)
    spread = jnp.mean(v * v, axis=0, keepdims=True) - center * center
    return (v - center) * lax.rsqrt(spread + 1e-05) * gain + offset


def columns(row):
    return jnp.broadcast_to(row, (128, 128)).T


def dot(a, b, dims=((1,), (0,))):
    return lax.dot_general(a, b, (dims, ((), ())), preferred_element_type=F32)


def kernel(
    pair, win, wgate, wout, pgain, pbias, hgain, hbias, cgain, mask, chain, out,
    pbuf, win_all, wgate_all, wout_t, mysmall, small_all, par, edge, turn, turn_lr,
    cur, normed, gate, stage, lr, tbuf, tri, obuf,
    p_send, p_recv, p_own, w_send, w_recv, w_own, lr_send, lr_recv, t_send, t_recv, o_send, o_recv, o_own, ready,
):
    r = lax.axis_index("rows")
    c = lax.axis_index("ch")
    x = lax.div(r, 8)
    zy = lax.rem(r, 8)
    y = lax.rem(zy, 4)
    spot = zy * 4 + c
    group = lax.rem(x + y, 4)
    mine = group * 32 + spot
    peers = [lax.rem(c + s, 4) for s in (1, 2, 3)]

    def place(turned, s):
        g = lax.rem(group + turned, 4)
        m = lax.rem(spot + s, 32)
        zy2 = lax.div(m, 4)
        x2 = lax.rem(g + 4 - lax.rem(zy2, 4), 4)
        return g * 32 + m, x2 * 8 + zy2, lax.rem(m, 4)

    barrier = pltpu.get_barrier_semaphore()
    for c2 in peers:
        pl.semaphore_signal(barrier, inc=1, device_id=(r, c2), device_id_type=MESH)

    @pl.loop(1, 32)
    def _(s):
        pl.semaphore_signal(barrier, inc=1, device_id=(lax.rem(r + s, 32), c), device_id_type=MESH)

    mysmall[...] = jnp.zeros_like(mysmall)
    mysmall[0:2, 0:32] = hgain[...]
    mysmall[2:4, 0:32] = hbias[...]
    mysmall[4:6, 0:32] = cgain[...]
    pl.semaphore_wait(barrier, 34)
    for c2 in peers:
        pl.semaphore_signal(ready, inc=1, device_id=(r, c2), device_id_type=MESH)

    def spread(k, src, dst, send, recv):
        copies = []
        for s, c2 in enumerate(peers):
            cp = pltpu.make_async_remote_copy(
                src_ref=src(c2), dst_ref=dst, send_sem=send.at[k, s], recv_sem=recv.at[k, s],
                device_id=(r, c2), device_id_type=MESH,
            )
            cp.start()
            copies.append(cp)
        return copies

    def own(k, src, dst, sem):
        cp = pltpu.make_async_copy(src, dst, sem.at[k])
        cp.start()
        return cp

    rows_c = aligned(c, 32)
    pair_c = lambda c2: pair.at[:, :, aligned(c2, 128)]
    moved = spread(0, pair_c, pbuf.at[rows_c], p_send, p_recv)
    moved_w0 = spread(0, lambda _: win.at[0], win_all.at[0, :, rows_c], w_send, w_recv)
    moved_sm = spread(1, lambda _: mysmall, small_all.at[c], w_send, w_recv)
    kept = own(0, pair_c(c), pbuf.at[rows_c], p_own)
    kept_w = [
        own(0, win.at[0], win_all.at[0, :, rows_c], w_own),
        own(1, mysmall, small_all.at[c], w_own),
        own(2, win.at[1], win_all.at[1, :, rows_c], w_own),
        own(3, wgate, wgate_all.at[:, rows_c], w_own),
    ]

    for u in range(2):
        par[u] = columns(pgain[u : u + 1, :])
        par[2 + u] = columns(pbias[u : u + 1, :])
        wout_t[u] = wout[u].astype(F32).T.astype(BF16)
    block = lax.div(r, 8)
    for k, ref in enumerate((mask, chain)):
        turn[128 * k : 128 * (k + 1), :] = columns(ref[pl.ds(block, 1), :].astype(F32))
    own_rows = lambda k: turn[pl.ds(pl.multiple_of(128 * k + lax.rem(r, 8) * 16, 16), 16), :]
    edge[0] = own_rows(0) * mask[pl.ds(c, 1), :].astype(F32)
    edge[1] = jnp.where(own_rows(1) != chain[pl.ds(c, 1), :].astype(F32), 1.0, 0.0)

    kept.wait()
    for cp in moved:
        cp.wait()
    turn[...] = pbuf[...].astype(F32).reshape(2048, 128)

    @pl.loop(0, 16)
    def _(i):
        v = turn[pl.ds(i, 128, stride=16), :]
        at = aligned(i, 128)
        cur[:, at] = v
        normed[:, at] = norm(v, par[0], par[2]).astype(BF16)

    for cp in kept_w[:2] + moved_sm:
        cp.wait()
    lanes = lax.broadcasted_iota(jnp.int32, (8, 128), 1)
    smalls = small_all[0]
    for c2 in (1, 2, 3):
        smalls = jnp.where(lanes >= 32 * c2, pltpu.roll(small_all[c2], 32 * c2, 1), smalls)
    for k in range(6):
        par[4 + k] = columns(smalls[k : k + 1, :])
    for cp in moved_w0:
        cp.wait()
    pl.semaphore_wait(ready, 3)

    later = []
    for u in range(2):
        @pl.loop(0, 4)
        def _(q, u=u):
            g = lax.rem(group + q, 4)
            rows_g = aligned(g, 32)
            weight = win_all[u, :, rows_g, :].reshape(128, 128)
            cross = par[8 + u, rows_g, :]

            @pl.loop(0, 8)
            def _(b):
                proj = dot(weight, normed[:, aligned(b, 256)])
                left = sigmoid(proj[0:32]) * proj[32:64]
                right = sigmoid(proj[64:96]) * proj[96:128]
                for k in range(2):
                    i = 2 * b + k
                    factor = edge[0, pl.ds(i, 1), :] * jnp.where(edge[1, pl.ds(i, 1), :] > 0.5, cross, 1.0)
                    half = slice(128 * k, 128 * (k + 1))
                    turn_lr[pl.ds(i, 32, stride=16), :] = factor * left[:, half]
                    turn_lr[pl.ds(512 + i, 32, stride=16), :] = factor * right[:, half]

            for k in range(2):
                stage[u, rows_g, k] = turn_lr[512 * k : 512 * (k + 1), :].astype(BF16).reshape(32, 16, 128)

            @pl.loop(jnp.where(q == 0, 1, 0), 32)
            def _(s):
                h2, r2, c2 = place(q, s)
                pltpu.make_async_remote_copy(
                    src_ref=stage.at[u, h2], dst_ref=lr.at[u, :, aligned(r, 16), aligned(c, 128)],
                    send_sem=lr_send.at[u], recv_sem=lr_recv.at[u], device_id=(r2, c2), device_id_type=MESH,
                ).start()

        pltpu.make_async_copy(
            stage.at[u, mine], lr.at[u, :, aligned(r, 16), aligned(c, 128)], lr_recv.at[u]
        ).start()
        if u == 0:
            moved_g = spread(2, lambda _: wgate, wgate_all.at[:, rows_c], w_send, w_recv)
            moved_w1 = spread(3, lambda _: win.at[1], win_all.at[1, :, rows_c], w_send, w_recv)
            for cp in kept_w[2:] + moved_g + moved_w1:
                cp.wait()

        @pl.loop(0, 8)
        def _(b, u=u):
            at = aligned(b, 256)
            gate[:, at] = sigmoid(dot(wgate_all[u], normed[:, at]))

        whole = pltpu.make_async_remote_copy(
            src_ref=stage.at[u, pl.ds(0, 127)], dst_ref=lr.at[u], send_sem=lr_send.at[u], recv_sem=lr_recv.at[u],
            device_id=(r, peers[0]), device_id_type=MESH,
        )
        whole.wait_recv()
        later.append(whole)

        @pl.loop(0, 4)
        def _(q, u=u):
            at = aligned(q, 128)
            if u == 0:
                part = dot(lr[u, 0, at, :], lr[u, 1], ((1,), (1,)))
            else:
                part = dot(lr[u, 0, :, at], lr[u, 1], ((0,), (0,)))
            tbuf[u, at, :] = part.astype(BF16)

        @pl.loop(0, 4)
        def _(q, u=u):
            @pl.loop(jnp.where(q == 0, 1, 0), 32)
            def _(s):
                _, r2, c2 = place(q, s)
                pltpu.make_async_remote_copy(
                    src_ref=tbuf.at[u, aligned(r2, 16), aligned(c2, 128)], dst_ref=tri.at[u, mine],
                    send_sem=t_send.at[u], recv_sem=t_recv.at[u], device_id=(r2, c2), device_id_type=MESH,
                ).start()

        pltpu.make_async_copy(
            tbuf.at[u, aligned(r, 16), aligned(c, 128)], tri.at[u, mine], t_recv.at[u]
        ).start()
        pltpu.make_async_remote_copy(
            src_ref=tri.at[u], dst_ref=tri.at[u], send_sem=t_send.at[u], recv_sem=t_recv.at[u],
            device_id=(r, peers[0]), device_id_type=MESH,
        ).wait_recv()
        later.append(
            pltpu.make_async_remote_copy(
                src_ref=tri.at[u, pl.ds(0, 127)], dst_ref=tri.at[u, pl.ds(0, 127)], send_sem=t_send.at[u],
                recv_sem=t_recv.at[u], device_id=(r, peers[0]), device_id_type=MESH,
            )
        )
        turn[...] = tri[u].astype(F32).reshape(2048, 128)

        @pl.loop(0, 8)
        def _(b, u=u):
            at = aligned(b, 256)
            halves = [
                norm(turn[pl.ds(2 * b + k, 128, stride=16), :], par[4 + u], par[6 + u]).astype(BF16) for k in range(2)
            ]
            update = dot(wout_t[u], jnp.concatenate(halves, axis=1))
            new = (cur[:, at] + gate[:, at] * update).astype(BF16).astype(F32)
            if u == 0:
                cur[:, at] = new
                for k in range(2):
                    at2 = aligned(2 * b + k, 128)
                    half = new[:, 128 * k : 128 * (k + 1)]
                    normed[:, at2] = norm(half, par[1], par[3]).astype(BF16)
            else:
                for k in range(2):
                    turn[pl.ds(2 * b + k, 128, stride=16), :] = new[:, 128 * k : 128 * (k + 1)]

    obuf[...] = turn[...].astype(BF16).reshape(128, 16, 128)
    here = out.at[:, :, aligned(c, 128)]
    last = spread(0, lambda c2: obuf.at[aligned(c2, 32)], here, o_send, o_recv)
    own(0, obuf.at[rows_c], here, o_own).wait()
    for cp in last:
        cp.wait()
    for cp in later:
        cp.wait_send()


def per_device(
    pair, residue_mask, chain_ids, pair_gain, pair_bias, in_weight, gate_weight,
    hidden_gain, hidden_bias, cross_gain, out_weight,
):
    dma = pltpu.SemaphoreType.DMA
    return pl.pallas_call(
        kernel,
        out_shape=jax.ShapeDtypeStruct((32, 16, 512), BF16),
        in_specs=[ANY, ANY, ANY] + [VM] * 8,
        out_specs=ANY,
        scratch_shapes=[
            pltpu.VMEM((128, 16, 128), BF16),
            pltpu.VMEM((2, 4, 128, 128), BF16),
            pltpu.VMEM((2, 128, 128), BF16),
            pltpu.VMEM((2, 128, 128), BF16),
            pltpu.VMEM((8, 128), F32),
            pltpu.VMEM((4, 8, 128), F32),
            pltpu.VMEM((10, 128, 128), F32),
            pltpu.VMEM((2, 16, 128), F32),
            pltpu.VMEM((2048, 128), F32),
            pltpu.VMEM((1024, 128), F32),
            pltpu.VMEM((128, 2048), F32),
            pltpu.VMEM((128, 2048), BF16),
            pltpu.VMEM((128, 2048), F32),
            pltpu.VMEM((2, 128, 2, 16, 128), BF16),
            pltpu.VMEM((2, 2, 512, 512), BF16),
            pltpu.VMEM((2, 512, 512), BF16),
            pltpu.VMEM((2, 128, 16, 128), BF16),
            pltpu.VMEM((128, 16, 128), BF16),
            dma((1, 3)), dma((1, 3)), dma((1,)),
            dma((4, 3)), dma((4, 3)), dma((4,)),
            dma((2,)), dma((2,)), dma((2,)), dma((2,)),
            dma((1, 3)), dma((1, 3)), dma((1,)),
            pltpu.SemaphoreType.REGULAR,
        ],
        compiler_params=pltpu.CompilerParams(
            collective_id=0, has_side_effects=True, vmem_limit_bytes=48 * 2**20
        ),
    )(
        pair,
        jnp.swapaxes(in_weight, 2, 3),
        jnp.swapaxes(gate_weight, 1, 2),
        out_weight,
        pair_gain, pair_bias, hidden_gain, hidden_bias, cross_gain,
        residue_mask.reshape(4, 128), chain_ids.reshape(4, 128),
    )


def solution(mesh):
    placed = (
        P("ch", "rows", None), P(), P(), P(), P(), P(None, None, None, "ch"), P(None, None, "ch"),
        P(None, "ch"), P(None, "ch"), P(None, "ch"), P(),
    )
    return jax.shard_map(
        per_device, mesh=mesh, in_specs=placed, out_specs=P("ch", "rows", None), check_vma=False
    )
```

```python
import jax
import jax.numpy as jnp
from jax import lax
from jax.experimental import pallas as pl
from jax.experimental.pallas import tpu as pltpu
from jax.sharding import PartitionSpec as P

MESH = pl.DeviceIdType.MESH
ANY = pl.BlockSpec(memory_space=pl.ANY)
F32 = jnp.float32
BF16 = jnp.bfloat16


def aligned(index, size):
    return pl.ds(pl.multiple_of(index * size, size), size)


def sigmoid(v):
    return 0.5 * jnp.tanh(0.5 * v) + 0.5


def norm(v, gain, offset):
    center = jnp.mean(v, axis=0, keepdims=True)
    spread = jnp.mean(v * v, axis=0, keepdims=True) - center * center
    return (v - center) * lax.rsqrt(spread + 1e-05) * gain + offset


def columns(row):
    return jnp.broadcast_to(row, (128, 128)).T


def dot(a, b, dims=((1,), (0,))):
    return lax.dot_general(a, b, (dims, ((), ())), preferred_element_type=F32)


def kernel(
    pair, win, wgate, wout_hbm, pgain_hbm, pbias_hbm, hgain_hbm, hbias_hbm, cgain_hbm, mask_hbm, chain_hbm, out,
    wout, pgain, pbias, hgain, hbias, cgain, mask, chain,
    pbuf, win_all, wgate_all, wout_t, mysmall, small_all, par, edge, turn, turn_lr,
    cur, normed, gate, stage, lr, tbuf, tri, obuf,
    p_send, p_recv, p_own, w_send, w_recv, w_own, lr_send, lr_recv, t_send, t_recv, o_send, o_recv, o_own, f_own, ready,
):
    r = lax.axis_index("rows")
    c = lax.axis_index("ch")
    x = lax.div(r, 8)
    zy = lax.rem(r, 8)
    y = lax.rem(zy, 4)
    spot = zy * 4 + c
    group = lax.rem(x + y, 4)
    mine = group * 32 + spot
    peers = [lax.rem(c + s, 4) for s in (1, 2, 3)]

    def place(turned, s):
        g = lax.rem(group + turned, 4)
        m = lax.rem(spot + s, 32)
        zy2 = lax.div(m, 4)
        x2 = lax.rem(g + 4 - lax.rem(zy2, 4), 4)
        return g * 32 + m, x2 * 8 + zy2, lax.rem(m, 4)

    fetched = [
        pltpu.make_async_copy(a, b, f_own.at[k])
        for k, (a, b) in enumerate((
            (hgain_hbm, hgain), (hbias_hbm, hbias), (cgain_hbm, cgain), (pgain_hbm, pgain),
            (pbias_hbm, pbias), (mask_hbm, mask), (chain_hbm, chain), (wout_hbm, wout),
        ))
    ]
    for cp in fetched:
        cp.start()
    barrier = pltpu.get_barrier_semaphore()
    for c2 in peers:
        pl.semaphore_signal(barrier, inc=1, device_id=(r, c2), device_id_type=MESH)

    @pl.loop(1, 32)
    def _(s):
        pl.semaphore_signal(barrier, inc=1, device_id=(lax.rem(r + s, 32), c), device_id_type=MESH)

    for cp in fetched[:3]:
        cp.wait()
    mysmall[...] = jnp.zeros_like(mysmall)
    mysmall[0:2, 0:32] = hgain[...]
    mysmall[2:4, 0:32] = hbias[...]
    mysmall[4:6, 0:32] = cgain[...]
    pl.semaphore_wait(barrier, 34)
    for c2 in peers:
        pl.semaphore_signal(ready, inc=1, device_id=(r, c2), device_id_type=MESH)

    def spread(k, src, dst, send, recv):
        copies = []
        for s, c2 in enumerate(peers):
            cp = pltpu.make_async_remote_copy(
                src_ref=src(c2), dst_ref=dst, send_sem=send.at[k, s], recv_sem=recv.at[k, s],
                device_id=(r, c2), device_id_type=MESH,
            )
            cp.start()
            copies.append(cp)
        return copies

    def own(k, src, dst, sem):
        cp = pltpu.make_async_copy(src, dst, sem.at[k])
        cp.start()
        return cp

    rows_c = aligned(c, 32)
    pair_c = lambda c2: pair.at[:, :, aligned(c2, 128)]
    moved = spread(0, pair_c, pbuf.at[rows_c], p_send, p_recv)
    moved_w0 = spread(0, lambda _: win.at[0], win_all.at[0, :, rows_c], w_send, w_recv)
    moved_sm = spread(1, lambda _: mysmall, small_all.at[c], w_send, w_recv)
    kept = own(0, pair_c(c), pbuf.at[rows_c], p_own)
    kept_w = [
        own(0, win.at[0], win_all.at[0, :, rows_c], w_own),
        own(1, mysmall, small_all.at[c], w_own),
        own(2, win.at[1], win_all.at[1, :, rows_c], w_own),
        own(3, wgate, wgate_all.at[:, rows_c], w_own),
    ]

    for cp in fetched[3:]:
        cp.wait()
    for u in range(2):
        par[u] = columns(pgain[u : u + 1, :])
        par[2 + u] = columns(pbias[u : u + 1, :])
        wout_t[u] = wout[u].astype(F32).T.astype(BF16)
    block = lax.div(r, 8)
    for k, ref in enumerate((mask, chain)):
        turn[128 * k : 128 * (k + 1), :] = columns(ref[pl.ds(block, 1), :].astype(F32))
    own_rows = lambda k: turn[pl.ds(pl.multiple_of(128 * k + lax.rem(r, 8) * 16, 16), 16), :]
    edge[0] = own_rows(0) * mask[pl.ds(c, 1), :].astype(F32)
    edge[1] = jnp.where(own_rows(1) != chain[pl.ds(c, 1), :].astype(F32), 1.0, 0.0)

    kept.wait()
    for cp in moved:
        cp.wait()
    turn[...] = pbuf[...].astype(F32).reshape(2048, 128)

    @pl.loop(0, 16)
    def _(i):
        v = turn[pl.ds(i, 128, stride=16), :]
        at = aligned(i, 128)
        cur[:, at] = v
        normed[:, at] = norm(v, par[0], par[2]).astype(BF16)

    for cp in kept_w[:2] + moved_sm:
        cp.wait()
    lanes = lax.broadcasted_iota(jnp.int32, (8, 128), 1)
    smalls = small_all[0]
    for c2 in (1, 2, 3):
        smalls = jnp.where(lanes >= 32 * c2, pltpu.roll(small_all[c2], 32 * c2, 1), smalls)
    for k in range(6):
        par[4 + k] = columns(smalls[k : k + 1, :])
    for cp in moved_w0:
        cp.wait()
    pl.semaphore_wait(ready, 3)

    later = []
    for u in range(2):
        @pl.loop(0, 4)
        def _(q, u=u):
            g = lax.rem(group + q, 4)
            rows_g = aligned(g, 32)
            weight = win_all[u, :, rows_g, :].reshape(128, 128)
            cross = par[8 + u, rows_g, :]

            @pl.loop(0, 8)
            def _(b):
                proj = dot(weight, normed[:, aligned(b, 256)])
                left = sigmoid(proj[0:32]) * proj[32:64]
                right = sigmoid(proj[64:96]) * proj[96:128]
                for k in range(2):
                    i = 2 * b + k
                    factor = edge[0, pl.ds(i, 1), :] * jnp.where(edge[1, pl.ds(i, 1), :] > 0.5, cross, 1.0)
                    half = slice(128 * k, 128 * (k + 1))
                    turn_lr[pl.ds(i, 32, stride=16), :] = factor * left[:, half]
                    turn_lr[pl.ds(512 + i, 32, stride=16), :] = factor * right[:, half]

            for k in range(2):
                stage[u, rows_g, k] = turn_lr[512 * k : 512 * (k + 1), :].astype(BF16).reshape(32, 16, 128)

            @pl.loop(jnp.where(q == 0, 1, 0), 32)
            def _(s):
                h2, r2, c2 = place(q, s)
                pltpu.make_async_remote_copy(
                    src_ref=stage.at[u, h2], dst_ref=lr.at[u, :, aligned(r, 16), aligned(c, 128)],
                    send_sem=lr_send.at[u], recv_sem=lr_recv.at[u], device_id=(r2, c2), device_id_type=MESH,
                ).start()

        pltpu.make_async_copy(
            stage.at[u, mine], lr.at[u, :, aligned(r, 16), aligned(c, 128)], lr_recv.at[u]
        ).start()
        if u == 0:
            moved_g = spread(2, lambda _: wgate, wgate_all.at[:, rows_c], w_send, w_recv)
            moved_w1 = spread(3, lambda _: win.at[1], win_all.at[1, :, rows_c], w_send, w_recv)
            for cp in kept_w[2:] + moved_g + moved_w1:
                cp.wait()

        @pl.loop(0, 8)
        def _(b, u=u):
            at = aligned(b, 256)
            gate[:, at] = sigmoid(dot(wgate_all[u], normed[:, at]))

        whole = pltpu.make_async_remote_copy(
            src_ref=stage.at[u, pl.ds(0, 127)], dst_ref=lr.at[u], send_sem=lr_send.at[u], recv_sem=lr_recv.at[u],
            device_id=(r, peers[0]), device_id_type=MESH,
        )
        whole.wait_recv()
        later.append(whole)

        @pl.loop(0, 4)
        def _(q, u=u):
            at = aligned(q, 128)
            if u == 0:
                part = dot(lr[u, 0, at, :], lr[u, 1], ((1,), (1,)))
            else:
                part = dot(lr[u, 0, :, at], lr[u, 1], ((0,), (0,)))
            tbuf[u, at, :] = part.astype(BF16)

        @pl.loop(0, 4)
        def _(q, u=u):
            @pl.loop(jnp.where(q == 0, 1, 0), 32)
            def _(s):
                _, r2, c2 = place(q, s)
                pltpu.make_async_remote_copy(
                    src_ref=tbuf.at[u, aligned(r2, 16), aligned(c2, 128)], dst_ref=tri.at[u, mine],
                    send_sem=t_send.at[u], recv_sem=t_recv.at[u], device_id=(r2, c2), device_id_type=MESH,
                ).start()

        pltpu.make_async_copy(
            tbuf.at[u, aligned(r, 16), aligned(c, 128)], tri.at[u, mine], t_recv.at[u]
        ).start()
        pltpu.make_async_remote_copy(
            src_ref=tri.at[u], dst_ref=tri.at[u], send_sem=t_send.at[u], recv_sem=t_recv.at[u],
            device_id=(r, peers[0]), device_id_type=MESH,
        ).wait_recv()
        later.append(
            pltpu.make_async_remote_copy(
                src_ref=tri.at[u, pl.ds(0, 127)], dst_ref=tri.at[u, pl.ds(0, 127)], send_sem=t_send.at[u],
                recv_sem=t_recv.at[u], device_id=(r, peers[0]), device_id_type=MESH,
            )
        )
        turn[...] = tri[u].astype(F32).reshape(2048, 128)

        @pl.loop(0, 8)
        def _(b, u=u):
            at = aligned(b, 256)
            halves = [
                norm(turn[pl.ds(2 * b + k, 128, stride=16), :], par[4 + u], par[6 + u]).astype(BF16) for k in range(2)
            ]
            update = dot(wout_t[u], jnp.concatenate(halves, axis=1))
            new = (cur[:, at] + gate[:, at] * update).astype(BF16).astype(F32)
            if u == 0:
                cur[:, at] = new
                for k in range(2):
                    at2 = aligned(2 * b + k, 128)
                    half = new[:, 128 * k : 128 * (k + 1)]
                    normed[:, at2] = norm(half, par[1], par[3]).astype(BF16)
            else:
                for k in range(2):
                    turn[pl.ds(2 * b + k, 128, stride=16), :] = new[:, 128 * k : 128 * (k + 1)]

    obuf[...] = turn[...].astype(BF16).reshape(128, 16, 128)
    here = out.at[:, :, aligned(c, 128)]
    last = spread(0, lambda c2: obuf.at[aligned(c2, 32)], here, o_send, o_recv)
    own(0, obuf.at[rows_c], here, o_own).wait()
    for cp in last:
        cp.wait()
    for cp in later:
        cp.wait_send()


def per_device(
    pair, residue_mask, chain_ids, pair_gain, pair_bias, in_weight, gate_weight,
    hidden_gain, hidden_bias, cross_gain, out_weight,
):
    dma = pltpu.SemaphoreType.DMA
    return pl.pallas_call(
        kernel,
        out_shape=jax.ShapeDtypeStruct((32, 16, 512), BF16),
        in_specs=[ANY] * 11,
        out_specs=ANY,
        scratch_shapes=[
            pltpu.VMEM((2, 128, 128), BF16),
            pltpu.VMEM((2, 128), F32),
            pltpu.VMEM((2, 128), F32),
            pltpu.VMEM((2, 32), F32),
            pltpu.VMEM((2, 32), F32),
            pltpu.VMEM((2, 32), F32),
            pltpu.VMEM((4, 128), jnp.int32),
            pltpu.VMEM((4, 128), jnp.int32),
            pltpu.VMEM((128, 16, 128), BF16),
            pltpu.VMEM((2, 4, 128, 128), BF16),
            pltpu.VMEM((2, 128, 128), BF16),
            pltpu.VMEM((2, 128, 128), BF16),
            pltpu.VMEM((8, 128), F32),
            pltpu.VMEM((4, 8, 128), F32),
            pltpu.VMEM((10, 128, 128), F32),
            pltpu.VMEM((2, 16, 128), F32),
            pltpu.VMEM((2048, 128), F32),
            pltpu.VMEM((1024, 128), F32),
            pltpu.VMEM((128, 2048), F32),
            pltpu.VMEM((128, 2048), BF16),
            pltpu.VMEM((128, 2048), F32),
            pltpu.VMEM((2, 128, 2, 16, 128), BF16),
            pltpu.VMEM((2, 2, 512, 512), BF16),
            pltpu.VMEM((2, 512, 512), BF16),
            pltpu.VMEM((2, 128, 16, 128), BF16),
            pltpu.VMEM((128, 16, 128), BF16),
            dma((1, 3)), dma((1, 3)), dma((1,)),
            dma((4, 3)), dma((4, 3)), dma((4,)),
            dma((2,)), dma((2,)), dma((2,)), dma((2,)),
            dma((1, 3)), dma((1, 3)), dma((1,)), dma((8,)),
            pltpu.SemaphoreType.REGULAR,
        ],
        compiler_params=pltpu.CompilerParams(
            collective_id=0, has_side_effects=True, vmem_limit_bytes=62 * 2**20
        ),
    )(
        pair,
        jnp.swapaxes(in_weight, 2, 3),
        jnp.swapaxes(gate_weight, 1, 2),
        out_weight,
        pair_gain, pair_bias, hidden_gain, hidden_bias, cross_gain,
        residue_mask.reshape(4, 128), chain_ids.reshape(4, 128),
    )


def solution(mesh):
    placed = (
        P("ch", "rows", None), P(), P(), P(), P(), P(None, None, None, "ch"), P(None, None, "ch"),
        P(None, "ch"), P(None, "ch"), P(None, "ch"), P(),
    )
    return jax.shard_map(
        per_device, mesh=mesh, in_specs=placed, out_specs=P("ch", "rows", None), check_vma=False
    )
```

```python
import jax
import jax.numpy as jnp
from jax import lax
from jax.experimental import pallas as pl
from jax.experimental.pallas import tpu as pltpu
from jax.sharding import PartitionSpec as P

MESH = pl.DeviceIdType.MESH
ANY = pl.BlockSpec(memory_space=pl.ANY)
F32 = jnp.float32
BF16 = jnp.bfloat16


def aligned(index, size):
    return pl.ds(pl.multiple_of(index * size, size), size)


def sigmoid(v):
    return 0.5 * jnp.tanh(0.5 * v) + 0.5


def norm(v, gain, offset):
    center = jnp.mean(v, axis=0, keepdims=True)
    spread = jnp.mean(v * v, axis=0, keepdims=True) - center * center
    return (v - center) * lax.rsqrt(spread + 1e-05) * gain + offset


def columns(row):
    return jnp.broadcast_to(row, (128, 128)).T


def dot(a, b, dims=((1,), (0,))):
    return lax.dot_general(a, b, (dims, ((), ())), preferred_element_type=F32)


def kernel(
    pair, win, wgate, wout_hbm, pgain_hbm, pbias_hbm, hgain_hbm, hbias_hbm, cgain_hbm, mask_hbm, chain_hbm, out,
    wout, pgain, pbias, hgain, hbias, cgain, mask, chain,
    pbuf, win_all, wgate_all, wout_t, mysmall, small_all, par, edge, turn, turn_lr,
    cur, normed, gate, stage, lr, tbuf, tri, obuf,
    p_send, p_recv, p_own, w_send, w_recv, w_own, lr_send, lr_recv, t_send, t_recv, o_send, o_recv, o_own, f_own, ready,
):
    r = lax.axis_index("rows")
    c = lax.axis_index("ch")
    x = lax.div(r, 8)
    zy = lax.rem(r, 8)
    y = lax.rem(zy, 4)
    spot = zy * 4 + c
    group = lax.rem(x + y, 4)
    mine = group * 32 + spot
    peers = [lax.rem(c + s, 4) for s in (1, 2, 3)]

    turned = [lax.rem(c + k, 4) for k in range(4)]

    def each(q, send):
        g = lax.rem(group + q, 4)

        def line(j, skip):
            zy2 = lax.rem(zy + j, 8)
            r2 = lax.rem(g + 4 - lax.rem(zy2, 4), 4) * 8 + zy2
            for k in range(skip, 4):
                send(g * 32 + zy2 * 4 + turned[k], r2, turned[k])

        line(0, 1 if q == 0 else 0)
        @pl.loop(1, 8)
        def _(j):
            line(j, 0)

    fetched = [
        pltpu.make_async_copy(a, b, f_own.at[k])
        for k, (a, b) in enumerate((
            (hgain_hbm, hgain), (hbias_hbm, hbias), (cgain_hbm, cgain), (pgain_hbm, pgain),
            (pbias_hbm, pbias), (mask_hbm, mask), (chain_hbm, chain), (wout_hbm, wout),
        ))
    ]
    for cp in fetched:
        cp.start()
    barrier = pltpu.get_barrier_semaphore()
    for c2 in peers:
        pl.semaphore_signal(barrier, inc=1, device_id=(r, c2), device_id_type=MESH)

    x_peers = [lax.rem(x + k, 4) * 8 + zy for k in (1, 2, 3)]
    y_peers = [r - y + lax.rem(y + k, 4) for k in (1, 2, 3)]
    z_peers = [x * 8 + lax.rem(zy + 4, 8)]
    for r2 in x_peers + y_peers + z_peers:
        pl.semaphore_signal(barrier, inc=1, device_id=(r2, c), device_id_type=MESH)

    for cp in fetched[:3]:
        cp.wait()
    mysmall[...] = jnp.zeros_like(mysmall)
    mysmall[0:2, 0:32] = hgain[...]
    mysmall[2:4, 0:32] = hbias[...]
    mysmall[4:6, 0:32] = cgain[...]
    pl.semaphore_wait(barrier, 10)

    def spread(k, src, dst, send, recv):
        copies = []
        for s, c2 in enumerate(peers):
            cp = pltpu.make_async_remote_copy(
                src_ref=src(c2), dst_ref=dst, send_sem=send.at[k, s], recv_sem=recv.at[k, s],
                device_id=(r, c2), device_id_type=MESH,
            )
            cp.start()
            copies.append(cp)
        return copies

    def own(k, src, dst, sem):
        cp = pltpu.make_async_copy(src, dst, sem.at[k])
        cp.start()
        return cp

    rows_c = aligned(c, 32)
    pair_c = lambda c2: pair.at[:, :, aligned(c2, 128)]
    moved = spread(0, pair_c, pbuf.at[rows_c], p_send, p_recv)
    moved_w0 = spread(0, lambda _: win.at[0], win_all.at[0, :, rows_c], w_send, w_recv)
    moved_sm = spread(1, lambda _: mysmall, small_all.at[c], w_send, w_recv)
    moved_g = spread(2, lambda _: wgate, wgate_all.at[:, rows_c], w_send, w_recv)
    moved_w1 = spread(3, lambda _: win.at[1], win_all.at[1, :, rows_c], w_send, w_recv)
    kept = own(0, pair_c(c), pbuf.at[rows_c], p_own)
    kept_w = [
        own(0, win.at[0], win_all.at[0, :, rows_c], w_own),
        own(1, mysmall, small_all.at[c], w_own),
        own(2, win.at[1], win_all.at[1, :, rows_c], w_own),
        own(3, wgate, wgate_all.at[:, rows_c], w_own),
    ]

    for k, known in enumerate((x_peers, y_peers, z_peers)):
        for r2 in known:
            pl.semaphore_signal(ready.at[k], inc=1, device_id=(r2, c), device_id_type=MESH)
        pl.semaphore_wait(ready.at[k], len(known))

    for cp in fetched[3:]:
        cp.wait()
    for u in range(2):
        par[u] = columns(pgain[u : u + 1, :])
        par[2 + u] = columns(pbias[u : u + 1, :])
        wout_t[u] = wout[u].astype(F32).T.astype(BF16)
    block = lax.div(r, 8)
    for k, ref in enumerate((mask, chain)):
        turn[128 * k : 128 * (k + 1), :] = columns(ref[pl.ds(block, 1), :].astype(F32))
    own_rows = lambda k: turn[pl.ds(pl.multiple_of(128 * k + lax.rem(r, 8) * 16, 16), 16), :]
    edge[0] = own_rows(0) * mask[pl.ds(c, 1), :].astype(F32)
    edge[1] = jnp.where(own_rows(1) != chain[pl.ds(c, 1), :].astype(F32), 1.0, 0.0)

    kept.wait()
    for cp in moved:
        cp.wait()
    turn[...] = pbuf[...].astype(F32).reshape(2048, 128)

    @pl.loop(0, 16, unroll=4)
    def _(i):
        v = turn[pl.ds(i, 128, stride=16), :]
        at = aligned(i, 128)
        cur[:, at] = v
        normed[:, at] = norm(v, par[0], par[2]).astype(BF16)

    for cp in kept_w[:2] + moved_sm:
        cp.wait()
    lanes = lax.broadcasted_iota(jnp.int32, (8, 128), 1)
    smalls = small_all[0]
    for c2 in (1, 2, 3):
        smalls = jnp.where(lanes >= 32 * c2, pltpu.roll(small_all[c2], 32 * c2, 1), smalls)
    for k in range(6):
        par[4 + k] = columns(smalls[k : k + 1, :])
    for cp in moved_w0:
        cp.wait()

    later = []
    for u in range(2):
        for q in range(4):
            g = lax.rem(group + q, 4)
            rows_g = aligned(g, 32)
            weight = win_all[u, :, rows_g, :].reshape(128, 128)
            cross = par[8 + u, rows_g, :]

            @pl.loop(0, 8, unroll=8)
            def _(b, u=u, weight=weight, cross=cross):
                proj = dot(weight, normed[:, aligned(b, 256)])
                left = sigmoid(proj[0:32]) * proj[32:64]
                right = sigmoid(proj[64:96]) * proj[96:128]
                for k in range(2):
                    i = 2 * b + k
                    factor = edge[0, pl.ds(i, 1), :] * jnp.where(edge[1, pl.ds(i, 1), :] > 0.5, cross, 1.0)
                    half = slice(128 * k, 128 * (k + 1))
                    turn_lr[pl.ds(i, 32, stride=16), :] = factor * left[:, half]
                    turn_lr[pl.ds(512 + i, 32, stride=16), :] = factor * right[:, half]

            for k in range(2):
                stage[u, rows_g, k] = turn_lr[512 * k : 512 * (k + 1), :].astype(BF16).reshape(32, 16, 128)

            def send_lr(h2, r2, c2, u=u):
                pltpu.make_async_remote_copy(
                    src_ref=stage.at[u, h2], dst_ref=lr.at[u, :, aligned(r, 16), aligned(c, 128)],
                    send_sem=lr_send.at[u], recv_sem=lr_recv.at[u], device_id=(r2, c2), device_id_type=MESH,
                ).start()

            each(q, send_lr)

        pltpu.make_async_copy(
            stage.at[u, mine], lr.at[u, :, aligned(r, 16), aligned(c, 128)], lr_recv.at[u]
        ).start()
        if u == 0:
            for cp in kept_w[2:] + moved_g + moved_w1:
                cp.wait()

        @pl.loop(0, 8, unroll=8)
        def _(b, u=u):
            at = aligned(b, 256)
            gate[:, at] = sigmoid(dot(wgate_all[u], normed[:, at]))

        whole = pltpu.make_async_remote_copy(
            src_ref=stage.at[u, pl.ds(0, 127)], dst_ref=lr.at[u], send_sem=lr_send.at[u], recv_sem=lr_recv.at[u],
            device_id=(r, peers[0]), device_id_type=MESH,
        )
        whole.wait_recv()
        later.append(whole)

        dims = ((1,), (1,)) if u == 0 else ((0,), (0,))
        tbuf[u] = dot(lr[u, 0], lr[u, 1], dims).astype(BF16)

        def send_t(_, r2, c2, u=u):
            pltpu.make_async_remote_copy(
                src_ref=tbuf.at[u, aligned(r2, 16), aligned(c2, 128)], dst_ref=tri.at[u, mine],
                send_sem=t_send.at[u], recv_sem=t_recv.at[u], device_id=(r2, c2), device_id_type=MESH,
            ).start()

        for q in range(4):
            each(q, send_t)

        pltpu.make_async_copy(
            tbuf.at[u, aligned(r, 16), aligned(c, 128)], tri.at[u, mine], t_recv.at[u]
        ).start()
        pltpu.make_async_remote_copy(
            src_ref=tri.at[u], dst_ref=tri.at[u], send_sem=t_send.at[u], recv_sem=t_recv.at[u],
            device_id=(r, peers[0]), device_id_type=MESH,
        ).wait_recv()
        later.append(
            pltpu.make_async_remote_copy(
                src_ref=tri.at[u, pl.ds(0, 127)], dst_ref=tri.at[u, pl.ds(0, 127)], send_sem=t_send.at[u],
                recv_sem=t_recv.at[u], device_id=(r, peers[0]), device_id_type=MESH,
            )
        )
        turn[...] = tri[u].astype(F32).reshape(2048, 128)

        @pl.loop(0, 8, unroll=8)
        def _(b, u=u):
            at = aligned(b, 256)
            halves = [
                norm(turn[pl.ds(2 * b + k, 128, stride=16), :], par[4 + u], par[6 + u]).astype(BF16) for k in range(2)
            ]
            update = dot(wout_t[u], jnp.concatenate(halves, axis=1))
            new = (cur[:, at] + gate[:, at] * update).astype(BF16).astype(F32)
            if u == 0:
                cur[:, at] = new
                for k in range(2):
                    at2 = aligned(2 * b + k, 128)
                    half = new[:, 128 * k : 128 * (k + 1)]
                    normed[:, at2] = norm(half, par[1], par[3]).astype(BF16)
            else:
                for k in range(2):
                    turn[pl.ds(2 * b + k, 128, stride=16), :] = new[:, 128 * k : 128 * (k + 1)]

    obuf[...] = turn[...].astype(BF16).reshape(128, 16, 128)
    here = out.at[:, :, aligned(c, 128)]
    last = spread(0, lambda c2: obuf.at[aligned(c2, 32)], here, o_send, o_recv)
    own(0, obuf.at[rows_c], here, o_own).wait()
    for cp in last:
        cp.wait()
    for cp in later:
        cp.wait_send()


def per_device(
    pair, residue_mask, chain_ids, pair_gain, pair_bias, in_weight, gate_weight,
    hidden_gain, hidden_bias, cross_gain, out_weight,
):
    dma = pltpu.SemaphoreType.DMA
    return pl.pallas_call(
        kernel,
        out_shape=jax.ShapeDtypeStruct((32, 16, 512), BF16),
        in_specs=[ANY] * 11,
        out_specs=ANY,
        scratch_shapes=[
            pltpu.VMEM((2, 128, 128), BF16),
            pltpu.VMEM((2, 128), F32),
            pltpu.VMEM((2, 128), F32),
            pltpu.VMEM((2, 32), F32),
            pltpu.VMEM((2, 32), F32),
            pltpu.VMEM((2, 32), F32),
            pltpu.VMEM((4, 128), jnp.int32),
            pltpu.VMEM((4, 128), jnp.int32),
            pltpu.VMEM((128, 16, 128), BF16),
            pltpu.VMEM((2, 4, 128, 128), BF16),
            pltpu.VMEM((2, 128, 128), BF16),
            pltpu.VMEM((2, 128, 128), BF16),
            pltpu.VMEM((8, 128), F32),
            pltpu.VMEM((4, 8, 128), F32),
            pltpu.VMEM((10, 128, 128), F32),
            pltpu.VMEM((2, 16, 128), F32),
            pltpu.VMEM((2048, 128), F32),
            pltpu.VMEM((1024, 128), F32),
            pltpu.VMEM((128, 2048), F32),
            pltpu.VMEM((128, 2048), BF16),
            pltpu.VMEM((128, 2048), F32),
            pltpu.VMEM((2, 128, 2, 16, 128), BF16),
            pltpu.VMEM((2, 2, 512, 512), BF16),
            pltpu.VMEM((2, 512, 512), BF16),
            pltpu.VMEM((2, 128, 16, 128), BF16),
            pltpu.VMEM((128, 16, 128), BF16),
            dma((1, 3)), dma((1, 3)), dma((1,)),
            dma((4, 3)), dma((4, 3)), dma((4,)),
            dma((2,)), dma((2,)), dma((2,)), dma((2,)),
            dma((1, 3)), dma((1, 3)), dma((1,)), dma((8,)),
            pltpu.SemaphoreType.REGULAR((3,)),
        ],
        compiler_params=pltpu.CompilerParams(
            collective_id=0, has_side_effects=True, vmem_limit_bytes=62 * 2**20
        ),
    )(
        pair,
        jnp.swapaxes(in_weight, 2, 3),
        jnp.swapaxes(gate_weight, 1, 2),
        out_weight,
        pair_gain, pair_bias, hidden_gain, hidden_bias, cross_gain,
        residue_mask.reshape(4, 128), chain_ids.reshape(4, 128),
    )


def solution(mesh):
    placed = (
        P("ch", "rows", None), P(), P(), P(), P(), P(None, None, None, "ch"), P(None, None, "ch"),
        P(None, "ch"), P(None, "ch"), P(None, "ch"), P(),
    )
    return jax.shard_map(
        per_device, mesh=mesh, in_specs=placed, out_specs=P("ch", "rows", None), check_vma=False
    )
```

```python
import functools

import jax
import jax.numpy as jnp
from jax import lax
from jax.experimental import pallas as pl
from jax.experimental.pallas import tpu as pltpu
from jax.sharding import PartitionSpec as P

MESH = pl.DeviceIdType.MESH
ANY = pl.BlockSpec(memory_space=pl.ANY)
F32 = jnp.float32
BF16 = jnp.bfloat16


def aligned(index, size):
    return pl.ds(pl.multiple_of(index * size, size), size)


def sigmoid(v):
    return 0.5 * jnp.tanh(0.5 * v) + 0.5


def norm(v, gain, offset):
    center = jnp.mean(v, axis=0, keepdims=True)
    spread = jnp.mean(v * v, axis=0, keepdims=True) - center * center
    return (v - center) * lax.rsqrt(spread + 1e-05) * gain + offset


def columns(row):
    return jnp.broadcast_to(row, (128, 128)).T


def dot(a, b, dims=((1,), (0,))):
    return lax.dot_general(a, b, (dims, ((), ())), preferred_element_type=F32)


def kernel(
    pair, win, wgate, wout_hbm, pgain_hbm, pbias_hbm, hgain_hbm, hbias_hbm, cgain_hbm, mask_hbm, chain_hbm, out,
    wout, pgain, pbias, hgain, hbias, cgain, mask, chain,
    pbuf, win_all, wgate_all, wout_t, mysmall, small_all, par, edge, turn, turn_lr,
    cur, normed, gate, stage, lr, tbuf, tri, obuf,
    p_send, p_recv, p_own, w_send, w_recv, w_own, lr_send, first_recv, second_recv, t_send, t_recv, o_send, o_recv, o_own, f_own, ready,
):
    r = lax.axis_index("rows")
    c = lax.axis_index("ch")
    x = lax.div(r, 8)
    zy = lax.rem(r, 8)
    y = lax.rem(zy, 4)
    spot = zy * 4 + c
    group = lax.rem(x + y, 4)
    mine = group * 32 + spot
    spot_row = group * 8 + zy
    peers = [lax.rem(c + s, 4) for s in (1, 2, 3)]

    turned = [lax.rem(c + k, 4) for k in range(4)]

    def each(g, send, skip=0):
        def line(j, skip):
            zy2 = lax.rem(zy + j, 8)
            r2 = lax.rem(g + 4 - lax.rem(zy2, 4), 4) * 8 + zy2
            for k in range(skip, 4):
                send(g * 32 + zy2 * 4 + turned[k], r2, turned[k])

        line(0, skip)

        @pl.loop(1, 8)
        def _(j):
            line(j, 0)

    def hidden_row(r2):
        zy2 = lax.rem(r2, 8)
        return lax.rem(lax.div(r2, 8) + zy2, 4) * 8 + zy2

    fetched = [
        pltpu.make_async_copy(a, b, f_own.at[k])
        for k, (a, b) in enumerate((
            (hgain_hbm, hgain), (hbias_hbm, hbias), (cgain_hbm, cgain), (pgain_hbm, pgain),
            (pbias_hbm, pbias), (mask_hbm, mask), (chain_hbm, chain), (wout_hbm, wout),
        ))
    ]
    for cp in fetched:
        cp.start()
    barrier = pltpu.get_barrier_semaphore()
    for c2 in peers:
        pl.semaphore_signal(barrier, inc=1, device_id=(r, c2), device_id_type=MESH)

    x_peers = [lax.rem(x + k, 4) * 8 + zy for k in (1, 2, 3)]
    y_peers = [r - y + lax.rem(y + k, 4) for k in (1, 2, 3)]
    z_peers = [x * 8 + lax.rem(zy + 4, 8)]
    for r2 in x_peers + y_peers + z_peers:
        pl.semaphore_signal(barrier, inc=1, device_id=(r2, c), device_id_type=MESH)

    for cp in fetched[:3]:
        cp.wait()
    mysmall[...] = jnp.zeros_like(mysmall)
    mysmall[0:2, 0:32] = hgain[...]
    mysmall[2:4, 0:32] = hbias[...]
    mysmall[4:6, 0:32] = cgain[...]
    pl.semaphore_wait(barrier, 10)

    def spread(k, src, dst, send, recv):
        copies = []
        for s, c2 in enumerate(peers):
            cp = pltpu.make_async_remote_copy(
                src_ref=src(c2), dst_ref=dst, send_sem=send.at[k, s], recv_sem=recv.at[k, s],
                device_id=(r, c2), device_id_type=MESH,
            )
            cp.start()
            copies.append(cp)
        return copies

    def own(k, src, dst, sem):
        cp = pltpu.make_async_copy(src, dst, sem.at[k])
        cp.start()
        return cp

    rows_c = aligned(c, 32)
    pair_c = lambda c2: pair.at[:, :, aligned(c2, 128)]
    moved = spread(0, pair_c, pbuf.at[rows_c], p_send, p_recv)
    moved_w0 = spread(0, lambda _: win.at[0], win_all.at[0, :, rows_c], w_send, w_recv)
    moved_sm = spread(1, lambda _: mysmall, small_all.at[c], w_send, w_recv)
    moved_g = spread(2, lambda _: wgate, wgate_all.at[:, rows_c], w_send, w_recv)
    moved_w1 = spread(3, lambda _: win.at[1], win_all.at[1, :, rows_c], w_send, w_recv)
    kept = own(0, pair_c(c), pbuf.at[rows_c], p_own)
    kept_w = [
        own(0, win.at[0], win_all.at[0, :, rows_c], w_own),
        own(1, mysmall, small_all.at[c], w_own),
        own(2, win.at[1], win_all.at[1, :, rows_c], w_own),
        own(3, wgate, wgate_all.at[:, rows_c], w_own),
    ]

    for k, known in enumerate((x_peers, y_peers, z_peers)):
        for r2 in known:
            pl.semaphore_signal(ready.at[k], inc=1, device_id=(r2, c), device_id_type=MESH)
        pl.semaphore_wait(ready.at[k], len(known))

    for cp in fetched[3:]:
        cp.wait()
    for u in range(2):
        par[u] = columns(pgain[u : u + 1, :])
        par[2 + u] = columns(pbias[u : u + 1, :])
        wout_t[u] = wout[u].astype(F32).T.astype(BF16)
    block = lax.div(r, 8)
    for k, ref in enumerate((mask, chain)):
        turn[128 * k : 128 * (k + 1), :] = columns(ref[pl.ds(block, 1), :].astype(F32))
    own_rows = lambda k: turn[pl.ds(pl.multiple_of(128 * k + lax.rem(r, 8) * 16, 16), 16), :]
    edge[0] = own_rows(0) * mask[pl.ds(c, 1), :].astype(F32)
    edge[1] = jnp.where(own_rows(1) != chain[pl.ds(c, 1), :].astype(F32), 1.0, 0.0)

    kept.wait()
    for cp in moved:
        cp.wait()
    turn[...] = pbuf[...].astype(F32).reshape(2048, 128)

    @pl.loop(0, 16, unroll=4)
    def _(i):
        v = turn[pl.ds(i, 128, stride=16), :]
        at = aligned(i, 128)
        cur[:, at] = v
        normed[:, at] = norm(v, par[0], par[2]).astype(BF16)

    for cp in kept_w[:2] + moved_sm:
        cp.wait()
    lanes = lax.broadcasted_iota(jnp.int32, (8, 128), 1)
    smalls = small_all[0]
    for c2 in (1, 2, 3):
        smalls = jnp.where(lanes >= 32 * c2, pltpu.roll(small_all[c2], 32 * c2, 1), smalls)
    for k in range(6):
        par[4 + k] = columns(smalls[k : k + 1, :])
    for cp in moved_w0:
        cp.wait()

    later = []

    def landing(u, k):
        row = spot_row if (u, k) == (0, 0) else r
        return lr.at[u, k, aligned(row, 16), aligned(c, 128)]

    def send_lr(u, k, sem, h2, r2, c2):
        pltpu.make_async_remote_copy(
            src_ref=stage.at[u, h2, k], dst_ref=landing(u, k), send_sem=lr_send.at[u], recv_sem=sem,
            device_id=(r2, c2), device_id_type=MESH,
        ).start()

    def arrived(src, dst, send, recv):
        return pltpu.make_async_remote_copy(
            src_ref=src, dst_ref=dst, send_sem=send, recv_sem=recv, device_id=(r, peers[0]), device_id_type=MESH
        )

    for u in range(2):
        first, second = (1, 0) if u == 0 else (0, 1)
        for q in range(4):
            g = lax.rem(group + q, 4)
            rows_g = aligned(g, 32)
            weight = win_all[u, :, rows_g, :].reshape(128, 128)
            cross = par[8 + u, rows_g, :]

            @pl.loop(0, 8, unroll=8)
            def _(b, u=u, weight=weight, cross=cross):
                proj = dot(weight, normed[:, aligned(b, 256)])
                left = sigmoid(proj[0:32]) * proj[32:64]
                right = sigmoid(proj[64:96]) * proj[96:128]
                for k in range(2):
                    i = 2 * b + k
                    factor = edge[0, pl.ds(i, 1), :] * jnp.where(edge[1, pl.ds(i, 1), :] > 0.5, cross, 1.0)
                    half = slice(128 * k, 128 * (k + 1))
                    turn_lr[pl.ds(i, 32, stride=16), :] = factor * left[:, half]
                    turn_lr[pl.ds(512 + i, 32, stride=16), :] = factor * right[:, half]

            for k in range(2):
                stage[u, rows_g, k] = turn_lr[512 * k : 512 * (k + 1), :].astype(BF16).reshape(32, 16, 128)

            each(g, functools.partial(send_lr, u, first, first_recv.at[u]), 1 if q == 0 else 0)

        for q in range(4):
            if u == 0:
                g = lax.rem(group + q, 4)
                each(g, functools.partial(send_lr, u, second, second_recv.at[u, q]), 1 if q == 0 else 0)
            else:
                @pl.loop(1 if q == 0 else 0, 32)
                def _(j, u=u, q=q):
                    r2 = lax.rem(r + j, 32)
                    send_lr(u, second, second_recv.at[u, q], hidden_row(r2) * 4 + turned[q], r2, turned[q])

        for k, sem in ((first, first_recv.at[u]), (second, second_recv.at[u, 0])):
            pltpu.make_async_copy(stage.at[u, mine, k], landing(u, k), sem).start()
        if u == 0:
            for cp in kept_w[2:] + moved_g + moved_w1:
                cp.wait()

        @pl.loop(0, 8, unroll=8)
        def _(b, u=u):
            at = aligned(b, 256)
            gate[:, at] = sigmoid(dot(wgate_all[u], normed[:, at]))

        arrived(lr.at[u, first], lr.at[u, first], lr_send.at[u], first_recv.at[u]).wait_recv()
        later.append(arrived(stage.at[u, pl.ds(0, 127)], stage.at[u, pl.ds(0, 127)], lr_send.at[u], first_recv.at[u]))

        def send_t(_, r2, c2, u=u):
            row = hidden_row(r2) if u == 0 else r2
            pltpu.make_async_remote_copy(
                src_ref=tbuf.at[u, aligned(row, 16), aligned(c2, 128)], dst_ref=tri.at[u, mine],
                send_sem=t_send.at[u], recv_sem=t_recv.at[u], device_id=(r2, c2), device_id_type=MESH,
            ).start()

        for q in range(4):
            if u == 0:
                g = lax.rem(group + 4 - q, 4)
                part = lr.at[0, 0, aligned(g, 128)]
                arrived(part, part, lr_send.at[u], second_recv.at[u, q]).wait_recv()
                tbuf[0, aligned(g, 128), :] = dot(part[...], lr[0, 1], ((1,), (1,))).astype(BF16)
                each(g, send_t, 1 if q == 0 else 0)
            else:
                c2 = lax.rem(c + 4 - q, 4)
                part = lr.at[1, 1, :, aligned(c2, 128)]
                arrived(part, part, lr_send.at[u], second_recv.at[u, q]).wait_recv()
                tbuf[1, :, aligned(c2, 128)] = dot(lr[1, 0], part[...], ((0,), (0,))).astype(BF16)

                @pl.loop(1 if q == 0 else 0, 32)
                def _(j, c2=c2, send_t=send_t):
                    send_t(None, lax.rem(r + j, 32), c2)

        pltpu.make_async_copy(
            tbuf.at[u, aligned(spot_row if u == 0 else r, 16), aligned(c, 128)], tri.at[u, mine], t_recv.at[u]
        ).start()
        pltpu.make_async_remote_copy(
            src_ref=tri.at[u], dst_ref=tri.at[u], send_sem=t_send.at[u], recv_sem=t_recv.at[u],
            device_id=(r, peers[0]), device_id_type=MESH,
        ).wait_recv()
        later.append(
            pltpu.make_async_remote_copy(
                src_ref=tri.at[u, pl.ds(0, 127)], dst_ref=tri.at[u, pl.ds(0, 127)], send_sem=t_send.at[u],
                recv_sem=t_recv.at[u], device_id=(r, peers[0]), device_id_type=MESH,
            )
        )
        turn[...] = tri[u].astype(F32).reshape(2048, 128)

        @pl.loop(0, 8, unroll=8)
        def _(b, u=u):
            at = aligned(b, 256)
            halves = [
                norm(turn[pl.ds(2 * b + k, 128, stride=16), :], par[4 + u], par[6 + u]).astype(BF16) for k in range(2)
            ]
            update = dot(wout_t[u], jnp.concatenate(halves, axis=1))
            new = (cur[:, at] + gate[:, at] * update).astype(BF16).astype(F32)
            if u == 0:
                cur[:, at] = new
                for k in range(2):
                    at2 = aligned(2 * b + k, 128)
                    half = new[:, 128 * k : 128 * (k + 1)]
                    normed[:, at2] = norm(half, par[1], par[3]).astype(BF16)
            else:
                for k in range(2):
                    turn[pl.ds(2 * b + k, 128, stride=16), :] = new[:, 128 * k : 128 * (k + 1)]

    obuf[...] = turn[...].astype(BF16).reshape(128, 16, 128)
    here = out.at[:, :, aligned(c, 128)]
    last = spread(0, lambda c2: obuf.at[aligned(c2, 32)], here, o_send, o_recv)
    own(0, obuf.at[rows_c], here, o_own).wait()
    for cp in last:
        cp.wait()
    for cp in later:
        cp.wait_send()


def per_device(
    pair, residue_mask, chain_ids, pair_gain, pair_bias, in_weight, gate_weight,
    hidden_gain, hidden_bias, cross_gain, out_weight,
):
    dma = pltpu.SemaphoreType.DMA
    return pl.pallas_call(
        kernel,
        out_shape=jax.ShapeDtypeStruct((32, 16, 512), BF16),
        in_specs=[ANY] * 11,
        out_specs=ANY,
        scratch_shapes=[
            pltpu.VMEM((2, 128, 128), BF16),
            pltpu.VMEM((2, 128), F32),
            pltpu.VMEM((2, 128), F32),
            pltpu.VMEM((2, 32), F32),
            pltpu.VMEM((2, 32), F32),
            pltpu.VMEM((2, 32), F32),
            pltpu.VMEM((4, 128), jnp.int32),
            pltpu.VMEM((4, 128), jnp.int32),
            pltpu.VMEM((128, 16, 128), BF16),
            pltpu.VMEM((2, 4, 128, 128), BF16),
            pltpu.VMEM((2, 128, 128), BF16),
            pltpu.VMEM((2, 128, 128), BF16),
            pltpu.VMEM((8, 128), F32),
            pltpu.VMEM((4, 8, 128), F32),
            pltpu.VMEM((10, 128, 128), F32),
            pltpu.VMEM((2, 16, 128), F32),
            pltpu.VMEM((2048, 128), F32),
            pltpu.VMEM((1024, 128), F32),
            pltpu.VMEM((128, 2048), F32),
            pltpu.VMEM((128, 2048), BF16),
            pltpu.VMEM((128, 2048), F32),
            pltpu.VMEM((2, 128, 2, 16, 128), BF16),
            pltpu.VMEM((2, 2, 512, 512), BF16),
            pltpu.VMEM((2, 512, 512), BF16),
            pltpu.VMEM((2, 128, 16, 128), BF16),
            pltpu.VMEM((128, 16, 128), BF16),
            dma((1, 3)), dma((1, 3)), dma((1,)),
            dma((4, 3)), dma((4, 3)), dma((4,)),
            dma((2,)), dma((2,)), dma((2, 4)), dma((2,)), dma((2,)),
            dma((1, 3)), dma((1, 3)), dma((1,)), dma((8,)),
            pltpu.SemaphoreType.REGULAR((3,)),
        ],
        compiler_params=pltpu.CompilerParams(
            collective_id=0, has_side_effects=True, vmem_limit_bytes=62 * 2**20
        ),
    )(
        pair,
        jnp.swapaxes(in_weight, 2, 3),
        jnp.swapaxes(gate_weight, 1, 2),
        out_weight,
        pair_gain, pair_bias, hidden_gain, hidden_bias, cross_gain,
        residue_mask.reshape(4, 128), chain_ids.reshape(4, 128),
    )


def solution(mesh):
    placed = (
        P("ch", "rows", None), P(), P(), P(), P(), P(None, None, None, "ch"), P(None, None, "ch"),
        P(None, "ch"), P(None, "ch"), P(None, "ch"), P(),
    )
    return jax.shard_map(
        per_device, mesh=mesh, in_specs=placed, out_specs=P("ch", "rows", None), check_vma=False
    )
```

```python
import functools

import jax
import jax.numpy as jnp
from jax import lax
from jax.experimental import pallas as pl
from jax.experimental.pallas import tpu as pltpu
from jax.sharding import PartitionSpec as P

MESH = pl.DeviceIdType.MESH
ANY = pl.BlockSpec(memory_space=pl.ANY)
F32 = jnp.float32
BF16 = jnp.bfloat16


def aligned(index, size):
    return pl.ds(pl.multiple_of(index * size, size), size)


def sigmoid(v):
    return 0.5 * jnp.tanh(0.5 * v) + 0.5


def norm(v, gain, offset):
    center = jnp.mean(v, axis=0, keepdims=True)
    spread = jnp.mean(v * v, axis=0, keepdims=True) - center * center
    return (v - center) * lax.rsqrt(spread + 1e-05) * gain + offset


def columns(row):
    return jnp.broadcast_to(row, (128, 128)).T


def dot(a, b, dims=((1,), (0,))):
    return lax.dot_general(a, b, (dims, ((), ())), preferred_element_type=F32)


def kernel(
    pair, win, wgate, wout_hbm, pgain_hbm, pbias_hbm, hgain_hbm, hbias_hbm, cgain_hbm, mask_hbm, chain_hbm, out,
    wout, pgain, pbias, hgain, hbias, cgain, mask, chain,
    pbuf, win_all, wgate_all, wout_t, mysmall, small_all, par, edge, turn, turn_lr,
    cur, normed, gate, stage, lr, tbuf, tri, obuf,
    p_send, p_recv, p_own, w_send, w_recv, w_own, lr_send, first_recv, second_recv, t_send, t_recv, o_send, o_recv, o_own, f_own, ready,
):
    r = lax.axis_index("rows")
    c = lax.axis_index("ch")
    x = lax.div(r, 8)
    zy = lax.rem(r, 8)
    y = lax.rem(zy, 4)
    spot = zy * 4 + c
    group = lax.rem(x + y, 4)
    mine = group * 32 + spot
    spot_row = group * 8 + zy
    peers = [lax.rem(c + s, 4) for s in (1, 2, 3)]

    turned = [lax.rem(c + k, 4) for k in range(4)]

    def each(g, send, skip=0):
        def line(j, skip):
            zy2 = lax.rem(zy + j, 8)
            r2 = lax.rem(g + 4 - lax.rem(zy2, 4), 4) * 8 + zy2
            for k in range(skip, 4):
                send(g * 32 + zy2 * 4 + turned[k], r2, turned[k])

        line(0, skip)

        @pl.loop(1, 8)
        def _(j):
            line(j, 0)

    def hidden_row(r2):
        zy2 = lax.rem(r2, 8)
        return lax.rem(lax.div(r2, 8) + zy2, 4) * 8 + zy2

    fetched = [
        pltpu.make_async_copy(a, b, f_own.at[k])
        for k, (a, b) in enumerate((
            (hgain_hbm, hgain), (hbias_hbm, hbias), (cgain_hbm, cgain), (pgain_hbm, pgain),
            (pbias_hbm, pbias), (mask_hbm, mask), (chain_hbm, chain), (wout_hbm, wout),
        ))
    ]
    for cp in fetched:
        cp.start()
    barrier = pltpu.get_barrier_semaphore()
    for c2 in peers:
        pl.semaphore_signal(barrier, inc=1, device_id=(r, c2), device_id_type=MESH)

    x_peers = [lax.rem(x + k, 4) * 8 + zy for k in (1, 2, 3)]
    y_peers = [r - y + lax.rem(y + k, 4) for k in (1, 2, 3)]
    z_peers = [x * 8 + lax.rem(zy + 4, 8)]
    for r2 in x_peers + y_peers + z_peers:
        pl.semaphore_signal(barrier, inc=1, device_id=(r2, c), device_id_type=MESH)
    core = lax.rem(c, 2)
    other = 2 - 2 * lax.div(c, 2)
    facing = [other + core, other + 1 - core]
    sibling = (r, 3 - other - core)
    across = [(z_peers[0], c2) for c2 in facing]
    w_peers = across + [sibling]
    for dev in across:
        pl.semaphore_signal(barrier, inc=1, device_id=dev, device_id_type=MESH)

    for cp in fetched[:3]:
        cp.wait()
    mysmall[...] = jnp.zeros_like(mysmall)
    mysmall[0:2, 0:32] = hgain[...]
    mysmall[2:4, 0:32] = hbias[...]
    mysmall[4:6, 0:32] = cgain[...]
    pl.semaphore_wait(barrier, 12)

    def spread(k, src, dst, send, recv, devices):
        copies = []
        for s, dev in enumerate(devices):
            cp = pltpu.make_async_remote_copy(
                src_ref=src(dev[1]), dst_ref=dst, send_sem=send.at[k, s], recv_sem=recv.at[k, s],
                device_id=dev, device_id_type=MESH,
            )
            cp.start()
            copies.append(cp)
        return copies

    def own(k, src, dst, sem):
        cp = pltpu.make_async_copy(src, dst, sem.at[k])
        cp.start()
        return cp

    rows_c = aligned(c, 32)
    c_peers = [(r, c2) for c2 in facing] + [sibling]
    pair_c = lambda c2: pair.at[:, :, aligned(c2, 128)]
    moved = spread(0, pair_c, pbuf.at[rows_c], p_send, p_recv, c_peers)
    moved_w0 = spread(0, lambda _: win.at[0], win_all.at[0, :, rows_c], w_send, w_recv, w_peers)
    moved_sm = spread(1, lambda _: mysmall, small_all.at[c], w_send, w_recv, w_peers)
    moved_g = spread(2, lambda _: wgate, wgate_all.at[:, rows_c], w_send, w_recv, w_peers)
    moved_w1 = spread(3, lambda _: win.at[1], win_all.at[1, :, rows_c], w_send, w_recv, w_peers)
    kept = own(0, pair_c(c), pbuf.at[rows_c], p_own)
    kept_w = [
        own(0, win.at[0], win_all.at[0, :, rows_c], w_own),
        own(1, mysmall, small_all.at[c], w_own),
        own(2, win.at[1], win_all.at[1, :, rows_c], w_own),
        own(3, wgate, wgate_all.at[:, rows_c], w_own),
    ]

    for k, known in enumerate((x_peers, y_peers, z_peers)):
        for r2 in known:
            pl.semaphore_signal(ready.at[k], inc=1, device_id=(r2, c), device_id_type=MESH)
        pl.semaphore_wait(ready.at[k], len(known))

    for cp in fetched[3:]:
        cp.wait()
    for u in range(2):
        par[u] = columns(pgain[u : u + 1, :])
        par[2 + u] = columns(pbias[u : u + 1, :])
        wout_t[u] = wout[u].astype(F32).T.astype(BF16)
    block = lax.div(r, 8)
    for k, ref in enumerate((mask, chain)):
        turn[128 * k : 128 * (k + 1), :] = columns(ref[pl.ds(block, 1), :].astype(F32))
    own_rows = lambda k: turn[pl.ds(pl.multiple_of(128 * k + lax.rem(r, 8) * 16, 16), 16), :]
    edge[0] = own_rows(0) * mask[pl.ds(c, 1), :].astype(F32)
    edge[1] = jnp.where(own_rows(1) != chain[pl.ds(c, 1), :].astype(F32), 1.0, 0.0)

    kept.wait()
    for cp in moved:
        cp.wait()
    turn[...] = pbuf[...].astype(F32).reshape(2048, 128)

    @pl.loop(0, 16, unroll=4)
    def _(i):
        v = turn[pl.ds(i, 128, stride=16), :]
        at = aligned(i, 128)
        cur[:, at] = v
        normed[:, at] = norm(v, par[0], par[2]).astype(BF16)

    for cp in kept_w[:2] + moved_sm:
        cp.wait()
    lanes = lax.broadcasted_iota(jnp.int32, (8, 128), 1)
    smalls = small_all[0]
    for c2 in (1, 2, 3):
        smalls = jnp.where(lanes >= 32 * c2, pltpu.roll(small_all[c2], 32 * c2, 1), smalls)
    for k in range(6):
        par[4 + k] = columns(smalls[k : k + 1, :])
    for cp in moved_w0:
        cp.wait()

    later = []

    def landing(u, k):
        row = spot_row if (u, k) == (0, 0) else r
        return lr.at[u, k, aligned(row, 16), aligned(c, 128)]

    def send_lr(u, k, sem, h2, r2, c2):
        pltpu.make_async_remote_copy(
            src_ref=stage.at[u, h2, k], dst_ref=landing(u, k), send_sem=lr_send.at[u], recv_sem=sem,
            device_id=(r2, c2), device_id_type=MESH,
        ).start()

    def arrived(src, dst, send, recv):
        return pltpu.make_async_remote_copy(
            src_ref=src, dst_ref=dst, send_sem=send, recv_sem=recv, device_id=(r, peers[0]), device_id_type=MESH
        )

    for u in range(2):
        first, second = (1, 0) if u == 0 else (0, 1)
        for q in range(4):
            g = lax.rem(group + q, 4)
            rows_g = aligned(g, 32)
            weight = win_all[u, :, rows_g, :].reshape(128, 128)
            cross = par[8 + u, rows_g, :]

            @pl.loop(0, 8, unroll=8)
            def _(b, u=u, weight=weight, cross=cross):
                proj = dot(weight, normed[:, aligned(b, 256)])
                left = sigmoid(proj[0:32]) * proj[32:64]
                right = sigmoid(proj[64:96]) * proj[96:128]
                for k in range(2):
                    i = 2 * b + k
                    factor = edge[0, pl.ds(i, 1), :] * jnp.where(edge[1, pl.ds(i, 1), :] > 0.5, cross, 1.0)
                    half = slice(128 * k, 128 * (k + 1))
                    turn_lr[pl.ds(i, 32, stride=16), :] = factor * left[:, half]
                    turn_lr[pl.ds(512 + i, 32, stride=16), :] = factor * right[:, half]

            for k in range(2):
                stage[u, rows_g, k] = turn_lr[512 * k : 512 * (k + 1), :].astype(BF16).reshape(32, 16, 128)

            each(g, functools.partial(send_lr, u, first, first_recv.at[u]), 1 if q == 0 else 0)

        for q in range(4):
            if u == 0:
                g = lax.rem(group + q, 4)
                each(g, functools.partial(send_lr, u, second, second_recv.at[u, q]), 1 if q == 0 else 0)
            else:
                @pl.loop(1 if q == 0 else 0, 32)
                def _(j, u=u, q=q):
                    r2 = lax.rem(r + j, 32)
                    send_lr(u, second, second_recv.at[u, q], hidden_row(r2) * 4 + turned[q], r2, turned[q])

        for k, sem in ((first, first_recv.at[u]), (second, second_recv.at[u, 0])):
            pltpu.make_async_copy(stage.at[u, mine, k], landing(u, k), sem).start()
        if u == 0:
            for cp in kept_w[2:] + moved_g + moved_w1:
                cp.wait()

        @pl.loop(0, 8, unroll=8)
        def _(b, u=u):
            at = aligned(b, 256)
            gate[:, at] = sigmoid(dot(wgate_all[u], normed[:, at]))

        arrived(lr.at[u, first], lr.at[u, first], lr_send.at[u], first_recv.at[u]).wait_recv()
        later.append(arrived(stage.at[u, pl.ds(0, 127)], stage.at[u, pl.ds(0, 127)], lr_send.at[u], first_recv.at[u]))

        def send_t(_, r2, c2, u=u):
            row = hidden_row(r2) if u == 0 else r2
            pltpu.make_async_remote_copy(
                src_ref=tbuf.at[u, aligned(row, 16), aligned(c2, 128)], dst_ref=tri.at[u, mine],
                send_sem=t_send.at[u], recv_sem=t_recv.at[u], device_id=(r2, c2), device_id_type=MESH,
            ).start()

        for q in range(4):
            if u == 0:
                g = lax.rem(group + 4 - q, 4)
                part = lr.at[0, 0, aligned(g, 128)]
                arrived(part, part, lr_send.at[u], second_recv.at[u, q]).wait_recv()
                tbuf[0, aligned(g, 128), :] = dot(part[...], lr[0, 1], ((1,), (1,))).astype(BF16)
                each(g, send_t, 1 if q == 0 else 0)
            else:
                c2 = lax.rem(c + 4 - q, 4)
                part = lr.at[1, 1, :, aligned(c2, 128)]
                arrived(part, part, lr_send.at[u], second_recv.at[u, q]).wait_recv()
                tbuf[1, :, aligned(c2, 128)] = dot(lr[1, 0], part[...], ((0,), (0,))).astype(BF16)

                @pl.loop(1 if q == 0 else 0, 32)
                def _(j, c2=c2, send_t=send_t):
                    send_t(None, lax.rem(r + j, 32), c2)

        pltpu.make_async_copy(
            tbuf.at[u, aligned(spot_row if u == 0 else r, 16), aligned(c, 128)], tri.at[u, mine], t_recv.at[u]
        ).start()
        pltpu.make_async_remote_copy(
            src_ref=tri.at[u], dst_ref=tri.at[u], send_sem=t_send.at[u], recv_sem=t_recv.at[u],
            device_id=(r, peers[0]), device_id_type=MESH,
        ).wait_recv()
        later.append(
            pltpu.make_async_remote_copy(
                src_ref=tri.at[u, pl.ds(0, 127)], dst_ref=tri.at[u, pl.ds(0, 127)], send_sem=t_send.at[u],
                recv_sem=t_recv.at[u], device_id=(r, peers[0]), device_id_type=MESH,
            )
        )
        turn[...] = tri[u].astype(F32).reshape(2048, 128)

        @pl.loop(0, 8, unroll=8)
        def _(b, u=u):
            at = aligned(b, 256)
            halves = [
                norm(turn[pl.ds(2 * b + k, 128, stride=16), :], par[4 + u], par[6 + u]).astype(BF16) for k in range(2)
            ]
            update = dot(wout_t[u], jnp.concatenate(halves, axis=1))
            new = (cur[:, at] + gate[:, at] * update).astype(BF16).astype(F32)
            if u == 0:
                cur[:, at] = new
                for k in range(2):
                    at2 = aligned(2 * b + k, 128)
                    half = new[:, 128 * k : 128 * (k + 1)]
                    normed[:, at2] = norm(half, par[1], par[3]).astype(BF16)
            else:
                for k in range(2):
                    turn[pl.ds(2 * b + k, 128, stride=16), :] = new[:, 128 * k : 128 * (k + 1)]

    obuf[...] = turn[...].astype(BF16).reshape(128, 16, 128)
    here = out.at[:, :, aligned(c, 128)]
    last = spread(0, lambda c2: obuf.at[aligned(c2, 32)], here, o_send, o_recv, c_peers)
    own(0, obuf.at[rows_c], here, o_own).wait()
    for cp in last:
        cp.wait()
    for cp in later:
        cp.wait_send()


def per_device(
    pair, residue_mask, chain_ids, pair_gain, pair_bias, in_weight, gate_weight,
    hidden_gain, hidden_bias, cross_gain, out_weight,
):
    dma = pltpu.SemaphoreType.DMA
    return pl.pallas_call(
        kernel,
        out_shape=jax.ShapeDtypeStruct((32, 16, 512), BF16),
        in_specs=[ANY] * 11,
        out_specs=ANY,
        scratch_shapes=[
            pltpu.VMEM((2, 128, 128), BF16),
            pltpu.VMEM((2, 128), F32),
            pltpu.VMEM((2, 128), F32),
            pltpu.VMEM((2, 32), F32),
            pltpu.VMEM((2, 32), F32),
            pltpu.VMEM((2, 32), F32),
            pltpu.VMEM((4, 128), jnp.int32),
            pltpu.VMEM((4, 128), jnp.int32),
            pltpu.VMEM((128, 16, 128), BF16),
            pltpu.VMEM((2, 4, 128, 128), BF16),
            pltpu.VMEM((2, 128, 128), BF16),
            pltpu.VMEM((2, 128, 128), BF16),
            pltpu.VMEM((8, 128), F32),
            pltpu.VMEM((4, 8, 128), F32),
            pltpu.VMEM((10, 128, 128), F32),
            pltpu.VMEM((2, 16, 128), F32),
            pltpu.VMEM((2048, 128), F32),
            pltpu.VMEM((1024, 128), F32),
            pltpu.VMEM((128, 2048), F32),
            pltpu.VMEM((128, 2048), BF16),
            pltpu.VMEM((128, 2048), F32),
            pltpu.VMEM((2, 128, 2, 16, 128), BF16),
            pltpu.VMEM((2, 2, 512, 512), BF16),
            pltpu.VMEM((2, 512, 512), BF16),
            pltpu.VMEM((2, 128, 16, 128), BF16),
            pltpu.VMEM((128, 16, 128), BF16),
            dma((1, 3)), dma((1, 3)), dma((1,)),
            dma((4, 3)), dma((4, 3)), dma((4,)),
            dma((2,)), dma((2,)), dma((2, 4)), dma((2,)), dma((2,)),
            dma((1, 3)), dma((1, 3)), dma((1,)), dma((8,)),
            pltpu.SemaphoreType.REGULAR((3,)),
        ],
        compiler_params=pltpu.CompilerParams(
            collective_id=0, has_side_effects=True, vmem_limit_bytes=62 * 2**20
        ),
    )(
        pair,
        jnp.swapaxes(in_weight, 2, 3),
        jnp.swapaxes(gate_weight, 1, 2),
        out_weight,
        pair_gain, pair_bias, hidden_gain, hidden_bias, cross_gain,
        residue_mask.reshape(4, 128), chain_ids.reshape(4, 128),
    )


def solution(mesh):
    placed = (
        P("ch", "rows", None), P(), P(), P(), P(), P(None, None, None, "ch"), P(None, None, "ch"),
        P(None, "ch"), P(None, "ch"), P(None, "ch"), P(),
    )
    return jax.shard_map(
        per_device, mesh=mesh, in_specs=placed, out_specs=P("ch", "rows", None), check_vma=False
    )
```

```python
import functools

import jax
import jax.numpy as jnp
from jax import lax
from jax.experimental import pallas as pl
from jax.experimental.pallas import tpu as pltpu
from jax.sharding import PartitionSpec as P

MESH = pl.DeviceIdType.MESH
ANY = pl.BlockSpec(memory_space=pl.ANY)
F32 = jnp.float32
BF16 = jnp.bfloat16


def aligned(index, size):
    return pl.ds(pl.multiple_of(index * size, size), size)


def sigmoid(v):
    return 0.5 * jnp.tanh(0.5 * v) + 0.5


def norm(v, gain, offset):
    center = jnp.mean(v, axis=0, keepdims=True)
    spread = jnp.mean(v * v, axis=0, keepdims=True) - center * center
    return (v - center) * lax.rsqrt(spread + 1e-05) * gain + offset


def twice(v):
    return jnp.concatenate([v, v], axis=1)


def columns(row):
    return jnp.broadcast_to(row, (128, 128)).T


def dot(a, b, dims=((1,), (0,))):
    return lax.dot_general(a, b, (dims, ((), ())), preferred_element_type=F32)


def kernel(
    pair, win, wgate, wout_hbm, pgain_hbm, pbias_hbm, hgain_hbm, hbias_hbm, cgain_hbm, mask_hbm, chain_hbm, out,
    wout, pgain, pbias, hgain, hbias, cgain, mask, chain,
    pbuf, win_all, wgate_all, wout_t, mysmall, small_all, par, edge, turn, turn_lr, turn_out,
    cur, normed, gate, stage, lr, tbuf, tri, obuf,
    p_send, p_recv, p_own, w_send, w_recv, w_own, lr_send, first_recv, second_recv, t_send, t_recv, o_send, o_recv, o_own, f_own, ready,
):
    r = lax.axis_index("rows")
    c = lax.axis_index("ch")
    x = lax.div(r, 8)
    zy = lax.rem(r, 8)
    y = lax.rem(zy, 4)
    spot = zy * 4 + c
    group = lax.rem(x + y, 4)
    mine = group * 32 + spot
    spot_row = group * 8 + zy
    peers = [lax.rem(c + s, 4) for s in (1, 2, 3)]

    turned = [lax.rem(c + k, 4) for k in range(4)]

    def each(g, send, skip=0):
        def line(j, skip):
            zy2 = lax.rem(zy + j, 8)
            r2 = lax.rem(g + 4 - lax.rem(zy2, 4), 4) * 8 + zy2
            for k in range(skip, 4):
                send(g * 32 + zy2 * 4 + turned[k], r2, turned[k])

        line(0, skip)

        @pl.loop(1, 8)
        def _(j):
            line(j, 0)

    def hidden_row(r2):
        zy2 = lax.rem(r2, 8)
        return lax.rem(lax.div(r2, 8) + zy2, 4) * 8 + zy2

    fetched = [
        pltpu.make_async_copy(a, b, f_own.at[k])
        for k, (a, b) in enumerate((
            (hgain_hbm, hgain), (hbias_hbm, hbias), (cgain_hbm, cgain), (pgain_hbm, pgain),
            (pbias_hbm, pbias), (mask_hbm, mask), (chain_hbm, chain), (wout_hbm, wout),
        ))
    ]
    for cp in fetched:
        cp.start()
    barrier = pltpu.get_barrier_semaphore()
    for c2 in peers:
        pl.semaphore_signal(barrier, inc=1, device_id=(r, c2), device_id_type=MESH)

    x_peers = [lax.rem(x + k, 4) * 8 + zy for k in (1, 2, 3)]
    y_peers = [r - y + lax.rem(y + k, 4) for k in (1, 2, 3)]
    z_peers = [x * 8 + lax.rem(zy + 4, 8)]
    for r2 in x_peers + y_peers + z_peers:
        pl.semaphore_signal(barrier, inc=1, device_id=(r2, c), device_id_type=MESH)
    core = lax.rem(c, 2)
    other = 2 - 2 * lax.div(c, 2)
    facing = [other + core, other + 1 - core]
    sibling = (r, 3 - other - core)
    across = [(z_peers[0], c2) for c2 in facing]
    w_peers = across + [sibling]
    for dev in across:
        pl.semaphore_signal(barrier, inc=1, device_id=dev, device_id_type=MESH)

    for cp in fetched[:3]:
        cp.wait()
    mysmall[...] = jnp.zeros_like(mysmall)
    mysmall[0:2, 0:32] = hgain[...]
    mysmall[2:4, 0:32] = hbias[...]
    mysmall[4:6, 0:32] = cgain[...]
    pl.semaphore_wait(barrier, 12)

    def spread(k, src, dst, send, recv, devices):
        copies = []
        for s, dev in enumerate(devices):
            cp = pltpu.make_async_remote_copy(
                src_ref=src(dev[1]), dst_ref=dst, send_sem=send.at[k, s], recv_sem=recv.at[k, s],
                device_id=dev, device_id_type=MESH,
            )
            cp.start()
            copies.append(cp)
        return copies

    def own(k, src, dst, sem):
        cp = pltpu.make_async_copy(src, dst, sem.at[k])
        cp.start()
        return cp

    rows_c = aligned(c, 32)
    c_peers = [(r, c2) for c2 in facing] + [sibling]
    pair_c = lambda c2: pair.at[:, :, aligned(c2, 128)]
    moved = spread(0, pair_c, pbuf.at[rows_c], p_send, p_recv, c_peers)
    moved_w0 = spread(0, lambda _: win.at[0], win_all.at[0, :, rows_c], w_send, w_recv, w_peers)
    moved_sm = spread(1, lambda _: mysmall, small_all.at[c], w_send, w_recv, w_peers)
    moved_g = spread(2, lambda _: wgate, wgate_all.at[:, rows_c], w_send, w_recv, w_peers)
    moved_w1 = spread(3, lambda _: win.at[1], win_all.at[1, :, rows_c], w_send, w_recv, w_peers)
    kept = own(0, pair_c(c), pbuf.at[rows_c], p_own)
    kept_w = [
        own(0, win.at[0], win_all.at[0, :, rows_c], w_own),
        own(1, mysmall, small_all.at[c], w_own),
        own(2, win.at[1], win_all.at[1, :, rows_c], w_own),
        own(3, wgate, wgate_all.at[:, rows_c], w_own),
    ]

    for k, known in enumerate((x_peers, y_peers, z_peers)):
        for r2 in known:
            pl.semaphore_signal(ready.at[k], inc=1, device_id=(r2, c), device_id_type=MESH)
        pl.semaphore_wait(ready.at[k], len(known))

    for cp in fetched[3:]:
        cp.wait()
    for u in range(2):
        par[u] = columns(pgain[u : u + 1, :])
        par[2 + u] = columns(pbias[u : u + 1, :])
        wout_t[u] = wout[u].astype(F32).T.astype(BF16)
    block = lax.div(r, 8)
    for k, ref in enumerate((mask, chain)):
        turn[128 * k : 128 * (k + 1), :] = columns(ref[pl.ds(block, 1), :].astype(F32))
    own_rows = lambda k: turn[pl.ds(pl.multiple_of(128 * k + lax.rem(r, 8) * 16, 16), 16), :]
    edge[0] = own_rows(0) * mask[pl.ds(c, 1), :].astype(F32)
    edge[1] = jnp.where(own_rows(1) != chain[pl.ds(c, 1), :].astype(F32), 1.0, 0.0)

    for cp in kept_w[:2] + moved_sm:
        cp.wait()
    lanes = lax.broadcasted_iota(jnp.int32, (8, 128), 1)
    smalls = small_all[0]
    for c2 in (1, 2, 3):
        smalls = jnp.where(lanes >= 32 * c2, pltpu.roll(small_all[c2], 32 * c2, 1), smalls)
    for k in range(6):
        par[4 + k] = columns(smalls[k : k + 1, :])
    for cp in moved_w0:
        cp.wait()

    def of_group(u, q):
        g = lax.rem(group + q, 4)
        rows_g = aligned(g, 32)
        return g, rows_g, win_all[u, :, rows_g, :].reshape(128, 128), par[8 + u, rows_g, :]

    def project(weight, cross, b, columns_b):
        proj = dot(weight, columns_b)
        left = sigmoid(proj[0:32]) * proj[32:64]
        right = sigmoid(proj[64:96]) * proj[96:128]
        for k in range(2):
            i = 2 * b + k
            factor = edge[0, pl.ds(i, 1), :] * jnp.where(edge[1, pl.ds(i, 1), :] > 0.5, cross, 1.0)
            half = slice(128 * k, 128 * (k + 1))
            turn_lr[pl.ds(i, 32, stride=16), :] = factor * left[:, half]
            turn_lr[pl.ds(512 + i, 32, stride=16), :] = factor * right[:, half]

    kept.wait()
    for cp in moved:
        cp.wait()
    turn[...] = pbuf[...].astype(F32).reshape(2048, 128)
    _, _, weight, cross = of_group(0, 0)

    @pl.loop(0, 8, unroll=8)
    def _(b, weight=weight, cross=cross):
        at = aligned(b, 256)
        v = jnp.concatenate([turn[pl.ds(2 * b + k, 128, stride=16), :] for k in range(2)], axis=1)
        cur[:, at] = v
        fresh = norm(v, twice(par[0]), twice(par[2])).astype(BF16)
        normed[:, at] = fresh
        project(weight, cross, b, fresh)

    later = []

    def tri_columns(u, b):
        v = jnp.concatenate([turn[pl.ds(2 * b + k, 128, stride=16), :] for k in range(2)], axis=1)
        return norm(v, twice(par[4 + u]), twice(par[6 + u])).astype(BF16)

    def landing(u, k):
        row = spot_row if (u, k) == (0, 0) else r
        return lr.at[u, k, aligned(row, 16), aligned(c, 128)]

    def send_lr(u, k, sem, h2, r2, c2):
        pltpu.make_async_remote_copy(
            src_ref=stage.at[u, h2, k], dst_ref=landing(u, k), send_sem=lr_send.at[u], recv_sem=sem,
            device_id=(r2, c2), device_id_type=MESH,
        ).start()

    def arrived(src, dst, send, recv):
        return pltpu.make_async_remote_copy(
            src_ref=src, dst_ref=dst, send_sem=send, recv_sem=recv, device_id=(r, peers[0]), device_id_type=MESH
        )

    for u in range(2):
        first, second = (1, 0) if u == 0 else (0, 1)
        for q in range(4):
            g, rows_g, weight, cross = of_group(u, q)
            if q > 0:

                @pl.loop(0, 8, unroll=8)
                def _(b, weight=weight, cross=cross):
                    project(weight, cross, b, normed[:, aligned(b, 256)])

            for k in range(2):
                stage[u, rows_g, k] = turn_lr[512 * k : 512 * (k + 1), :].astype(BF16).reshape(32, 16, 128)

            each(g, functools.partial(send_lr, u, first, first_recv.at[u]), 1 if q == 0 else 0)

        for q in range(4):
            if u == 0:
                g = lax.rem(group + q, 4)
                each(g, functools.partial(send_lr, u, second, second_recv.at[u, q]), 1 if q == 0 else 0)
            else:
                @pl.loop(1 if q == 0 else 0, 32)
                def _(j, u=u, q=q):
                    r2 = lax.rem(r + j, 32)
                    send_lr(u, second, second_recv.at[u, q], hidden_row(r2) * 4 + turned[q], r2, turned[q])

        for k, sem in ((first, first_recv.at[u]), (second, second_recv.at[u, 0])):
            pltpu.make_async_copy(stage.at[u, mine, k], landing(u, k), sem).start()
        if u == 0:
            for cp in kept_w[2:] + moved_g + moved_w1:
                cp.wait()

        @pl.loop(0, 8, unroll=8)
        def _(b, u=u):
            at = aligned(b, 256)
            gate[:, at] = sigmoid(dot(wgate_all[u], normed[:, at]))

        arrived(lr.at[u, first], lr.at[u, first], lr_send.at[u], first_recv.at[u]).wait_recv()
        later.append(arrived(stage.at[u, pl.ds(0, 127)], stage.at[u, pl.ds(0, 127)], lr_send.at[u], first_recv.at[u]))

        def send_t(_, r2, c2, u=u):
            row = hidden_row(r2) if u == 0 else r2
            pltpu.make_async_remote_copy(
                src_ref=tbuf.at[u, aligned(row, 16), aligned(c2, 128)], dst_ref=tri.at[u, mine],
                send_sem=t_send.at[u], recv_sem=t_recv.at[u], device_id=(r2, c2), device_id_type=MESH,
            ).start()

        for q in range(4):
            if u == 0:
                g = lax.rem(group + 4 - q, 4)
                part = lr.at[0, 0, aligned(g, 128)]
                arrived(part, part, lr_send.at[u], second_recv.at[u, q]).wait_recv()
                tbuf[0, aligned(g, 128), :] = dot(part[...], lr[0, 1], ((1,), (1,))).astype(BF16)
                each(g, send_t, 1 if q == 0 else 0)
            else:
                c2 = lax.rem(c + 4 - q, 4)
                part = lr.at[1, 1, :, aligned(c2, 128)]
                arrived(part, part, lr_send.at[u], second_recv.at[u, q]).wait_recv()
                tbuf[1, :, aligned(c2, 128)] = dot(lr[1, 0], part[...], ((0,), (0,))).astype(BF16)

                @pl.loop(1 if q == 0 else 0, 32)
                def _(j, c2=c2, send_t=send_t):
                    send_t(None, lax.rem(r + j, 32), c2)

        pltpu.make_async_copy(
            tbuf.at[u, aligned(spot_row if u == 0 else r, 16), aligned(c, 128)], tri.at[u, mine], t_recv.at[u]
        ).start()
        pltpu.make_async_remote_copy(
            src_ref=tri.at[u], dst_ref=tri.at[u], send_sem=t_send.at[u], recv_sem=t_recv.at[u],
            device_id=(r, peers[0]), device_id_type=MESH,
        ).wait_recv()
        later.append(
            pltpu.make_async_remote_copy(
                src_ref=tri.at[u, pl.ds(0, 127)], dst_ref=tri.at[u, pl.ds(0, 127)], send_sem=t_send.at[u],
                recv_sem=t_recv.at[u], device_id=(r, peers[0]), device_id_type=MESH,
            )
        )
        turn[...] = tri[u].astype(F32).reshape(2048, 128)

        if u == 0:
            _, _, weight, cross = of_group(1, 0)

            @pl.loop(0, 8, unroll=8)
            def _(b, weight=weight, cross=cross):
                at = aligned(b, 256)
                update = dot(wout_t[0], tri_columns(0, b))
                new = (cur[:, at] + gate[:, at] * update).astype(BF16).astype(F32)
                cur[:, at] = new
                fresh = norm(new, twice(par[1]), twice(par[3])).astype(BF16)
                normed[:, at] = fresh
                project(weight, cross, b, fresh)

    here = out.at[:, :, aligned(c, 128)]
    last = []
    for turned_half in range(2):
        half = lax.rem(lax.div(c, 2) + 1 + turned_half, 2)
        rows_h = aligned(half, 64)

        @pl.loop(0, 8, unroll=8)
        def _(b, first_half=turned_half == 0, half=half, rows_h=rows_h):
            at = aligned(b, 256)
            if first_half:
                normed[:, at] = tri_columns(1, b)
            update = dot(wout_t[1, rows_h, :], normed[:, at])
            new = cur[rows_h, at] + gate[rows_h, at] * update
            for k in range(2):
                turn_out[pl.ds(2 * b + k, 64, stride=16), :] = new[:, 128 * k : 128 * (k + 1)]

        obuf[rows_h] = turn_out[...].astype(BF16).reshape(64, 16, 128)
        for s in range(2) if turned_half == 0 else (2,):
            c2 = c_peers[s][1]
            cp = pltpu.make_async_remote_copy(
                src_ref=obuf.at[aligned(c2, 32)], dst_ref=here, send_sem=o_send.at[0, s], recv_sem=o_recv.at[0, s],
                device_id=c_peers[s], device_id_type=MESH,
            )
            cp.start()
            last.append(cp)
    own(0, obuf.at[rows_c], here, o_own).wait()
    for cp in last:
        cp.wait()
    for cp in later:
        cp.wait_send()


def per_device(
    pair, residue_mask, chain_ids, pair_gain, pair_bias, in_weight, gate_weight,
    hidden_gain, hidden_bias, cross_gain, out_weight,
):
    dma = pltpu.SemaphoreType.DMA
    return pl.pallas_call(
        kernel,
        out_shape=jax.ShapeDtypeStruct((32, 16, 512), BF16),
        in_specs=[ANY] * 11,
        out_specs=ANY,
        scratch_shapes=[
            pltpu.VMEM((2, 128, 128), BF16),
            pltpu.VMEM((2, 128), F32),
            pltpu.VMEM((2, 128), F32),
            pltpu.VMEM((2, 32), F32),
            pltpu.VMEM((2, 32), F32),
            pltpu.VMEM((2, 32), F32),
            pltpu.VMEM((4, 128), jnp.int32),
            pltpu.VMEM((4, 128), jnp.int32),
            pltpu.VMEM((128, 16, 128), BF16),
            pltpu.VMEM((2, 4, 128, 128), BF16),
            pltpu.VMEM((2, 128, 128), BF16),
            pltpu.VMEM((2, 128, 128), BF16),
            pltpu.VMEM((8, 128), F32),
            pltpu.VMEM((4, 8, 128), F32),
            pltpu.VMEM((10, 128, 128), F32),
            pltpu.VMEM((2, 16, 128), F32),
            pltpu.VMEM((2048, 128), F32),
            pltpu.VMEM((1024, 128), F32),
            pltpu.VMEM((1024, 128), F32),
            pltpu.VMEM((128, 2048), F32),
            pltpu.VMEM((128, 2048), BF16),
            pltpu.VMEM((128, 2048), F32),
            pltpu.VMEM((2, 128, 2, 16, 128), BF16),
            pltpu.VMEM((2, 2, 512, 512), BF16),
            pltpu.VMEM((2, 512, 512), BF16),
            pltpu.VMEM((2, 128, 16, 128), BF16),
            pltpu.VMEM((128, 16, 128), BF16),
            dma((1, 3)), dma((1, 3)), dma((1,)),
            dma((4, 3)), dma((4, 3)), dma((4,)),
            dma((2,)), dma((2,)), dma((2, 4)), dma((2,)), dma((2,)),
            dma((1, 3)), dma((1, 3)), dma((1,)), dma((8,)),
            pltpu.SemaphoreType.REGULAR((3,)),
        ],
        compiler_params=pltpu.CompilerParams(
            collective_id=0, has_side_effects=True, vmem_limit_bytes=62 * 2**20
        ),
    )(
        pair,
        jnp.swapaxes(in_weight, 2, 3),
        jnp.swapaxes(gate_weight, 1, 2),
        out_weight,
        pair_gain, pair_bias, hidden_gain, hidden_bias, cross_gain,
        residue_mask.reshape(4, 128), chain_ids.reshape(4, 128),
    )


def solution(mesh):
    placed = (
        P("ch", "rows", None), P(), P(), P(), P(), P(None, None, None, "ch"), P(None, None, "ch"),
        P(None, "ch"), P(None, "ch"), P(None, "ch"), P(),
    )
    return jax.shard_map(
        per_device, mesh=mesh, in_specs=placed, out_specs=P("ch", "rows", None), check_vma=False
    )
```

```python
import functools

import jax
import jax.numpy as jnp
from jax import lax
from jax.experimental import pallas as pl
from jax.experimental.pallas import tpu as pltpu
from jax.sharding import PartitionSpec as P

MESH = pl.DeviceIdType.MESH
ANY = pl.BlockSpec(memory_space=pl.ANY)
F32 = jnp.float32
BF16 = jnp.bfloat16


def aligned(index, size):
    return pl.ds(pl.multiple_of(index * size, size), size)


def sigmoid(v):
    return 0.5 * jnp.tanh(0.5 * v) + 0.5


def norm(v, gain, offset):
    center = jnp.mean(v, axis=0, keepdims=True)
    spread = jnp.mean(v * v, axis=0, keepdims=True) - center * center
    return (v - center) * lax.rsqrt(spread + 1e-05) * gain + offset


def twice(v):
    return jnp.concatenate([v, v], axis=1)


def columns(row):
    return jnp.broadcast_to(row, (128, 128)).T


def dot(a, b, dims=((1,), (0,))):
    return lax.dot_general(a, b, (dims, ((), ())), preferred_element_type=F32)


def kernel(
    pair, win, wgate, wout_hbm, pgain_hbm, pbias_hbm, hgain_hbm, hbias_hbm, cgain_hbm, mask_hbm, chain_hbm, out,
    wout, pgain, pbias, hgain, hbias, cgain, mask, chain,
    pbuf, win_all, wgate_all, wout_t, mysmall, small_all, par, edge, turn, turn_lr, turn_out,
    cur, normed, gate, stage, lr, tbuf, tri, obuf,
    p_send, p_recv, p_own, w_send, w_recv, w_own, lr_send, first_recv, second_recv, t_send, t_recv, o_send, o_recv, o_own, f_own, ready,
):
    r = lax.axis_index("rows")
    c = lax.axis_index("ch")
    x = lax.div(r, 8)
    zy = lax.rem(r, 8)
    y = lax.rem(zy, 4)
    spot = zy * 4 + c
    group = lax.rem(x + y, 4)
    mine = group * 32 + spot
    spot_row = group * 8 + zy
    peers = [lax.rem(c + s, 4) for s in (1, 2, 3)]

    turned = [lax.rem(c + k, 4) for k in range(4)]

    def each(g, send, skip=0):
        def line(j, skip):
            zy2 = lax.rem(zy + j, 8)
            r2 = lax.rem(g + 4 - lax.rem(zy2, 4), 4) * 8 + zy2
            for k in range(skip, 4):
                send(g * 32 + zy2 * 4 + turned[k], r2, turned[k])

        line(0, skip)

        @pl.loop(1, 8)
        def _(j):
            line(j, 0)

    def hidden_row(r2):
        zy2 = lax.rem(r2, 8)
        return lax.rem(lax.div(r2, 8) + zy2, 4) * 8 + zy2

    fetched = [
        pltpu.make_async_copy(a, b, f_own.at[k])
        for k, (a, b) in enumerate((
            (hgain_hbm, hgain), (hbias_hbm, hbias), (cgain_hbm, cgain), (pgain_hbm, pgain),
            (pbias_hbm, pbias), (mask_hbm, mask), (chain_hbm, chain), (wout_hbm, wout),
        ))
    ]
    for cp in fetched:
        cp.start()
    barrier = pltpu.get_barrier_semaphore()
    for c2 in peers:
        pl.semaphore_signal(barrier, inc=1, device_id=(r, c2), device_id_type=MESH)

    x_peers = [lax.rem(x + k, 4) * 8 + zy for k in (1, 2, 3)]
    y_peers = [r - y + lax.rem(y + k, 4) for k in (1, 2, 3)]
    z_peers = [x * 8 + lax.rem(zy + 4, 8)]
    for r2 in x_peers + y_peers + z_peers:
        pl.semaphore_signal(barrier, inc=1, device_id=(r2, c), device_id_type=MESH)
    core = lax.rem(c, 2)
    other = 2 - 2 * lax.div(c, 2)
    facing = [other + core, other + 1 - core]
    sibling = (r, 3 - other - core)
    across = [(z_peers[0], c2) for c2 in facing]
    w_peers = across + [sibling]
    for dev in across:
        pl.semaphore_signal(barrier, inc=1, device_id=dev, device_id_type=MESH)

    for cp in fetched[:3]:
        cp.wait()
    mysmall[...] = jnp.zeros_like(mysmall)
    mysmall[0:2, 0:32] = hgain[...]
    mysmall[2:4, 0:32] = hbias[...]
    mysmall[4:6, 0:32] = cgain[...]
    pl.semaphore_wait(barrier, 12)

    def spread(k, src, dst, send, recv, devices):
        copies = []
        for s, dev in enumerate(devices):
            cp = pltpu.make_async_remote_copy(
                src_ref=src(dev[1]), dst_ref=dst, send_sem=send.at[k, s], recv_sem=recv.at[k, s],
                device_id=dev, device_id_type=MESH,
            )
            cp.start()
            copies.append(cp)
        return copies

    def own(k, src, dst, sem):
        cp = pltpu.make_async_copy(src, dst, sem.at[k])
        cp.start()
        return cp

    rows_c = aligned(c, 32)
    c_peers = [(r, c2) for c2 in facing] + [sibling]
    pair_c = lambda c2: pair.at[:, :, aligned(c2, 128)]
    moved = spread(0, pair_c, pbuf.at[rows_c], p_send, p_recv, c_peers)
    moved_w0 = spread(0, lambda _: win.at[0], win_all.at[0, :, rows_c], w_send, w_recv, w_peers)
    moved_sm = spread(1, lambda _: mysmall, small_all.at[c], w_send, w_recv, w_peers)
    moved_g = spread(2, lambda _: wgate, wgate_all.at[:, rows_c], w_send, w_recv, w_peers)
    moved_w1 = spread(3, lambda _: win.at[1], win_all.at[1, :, rows_c], w_send, w_recv, w_peers)
    kept = own(0, pair_c(c), pbuf.at[rows_c], p_own)
    kept_w = [
        own(0, win.at[0], win_all.at[0, :, rows_c], w_own),
        own(1, mysmall, small_all.at[c], w_own),
        own(2, win.at[1], win_all.at[1, :, rows_c], w_own),
        own(3, wgate, wgate_all.at[:, rows_c], w_own),
    ]

    for k, known in enumerate((x_peers, y_peers, z_peers)):
        for r2 in known:
            pl.semaphore_signal(ready.at[k], inc=1, device_id=(r2, c), device_id_type=MESH)
        pl.semaphore_wait(ready.at[k], len(known))

    for cp in fetched[3:]:
        cp.wait()
    for u in range(2):
        par[u] = columns(pgain[u : u + 1, :])
        par[2 + u] = columns(pbias[u : u + 1, :])
        wout_t[u] = wout[u].astype(F32).T.astype(BF16)
    block = lax.div(r, 8)
    for k, ref in enumerate((mask, chain)):
        turn[128 * k : 128 * (k + 1), :] = columns(ref[pl.ds(block, 1), :].astype(F32))
    own_rows = lambda k: turn[pl.ds(pl.multiple_of(128 * k + lax.rem(r, 8) * 16, 16), 16), :]
    edge[0] = own_rows(0) * mask[pl.ds(c, 1), :].astype(F32)
    edge[1] = jnp.where(own_rows(1) != chain[pl.ds(c, 1), :].astype(F32), 1.0, 0.0)

    for cp in kept_w[:2] + moved_sm:
        cp.wait()
    lanes = lax.broadcasted_iota(jnp.int32, (8, 128), 1)
    smalls = small_all[0]
    for c2 in (1, 2, 3):
        smalls = jnp.where(lanes >= 32 * c2, pltpu.roll(small_all[c2], 32 * c2, 1), smalls)
    for k in range(6):
        par[4 + k] = columns(smalls[k : k + 1, :])
    for cp in moved_w0:
        cp.wait()

    def of_group(u, q):
        g = lax.rem(group + q, 4)
        rows_g = aligned(g, 32)
        return g, rows_g, win_all[u, :, rows_g, :].reshape(128, 128), par[8 + u, rows_g, :]

    def project(weight, cross, b, columns_b):
        proj = dot(weight, columns_b)
        left = sigmoid(proj[0:32]) * proj[32:64]
        right = sigmoid(proj[64:96]) * proj[96:128]
        for k in range(2):
            i = 2 * b + k
            factor = edge[0, pl.ds(i, 1), :] * jnp.where(edge[1, pl.ds(i, 1), :] > 0.5, cross, 1.0)
            half = slice(128 * k, 128 * (k + 1))
            turn_lr[pl.ds(i, 32, stride=16), :] = factor * left[:, half]
            turn_lr[pl.ds(512 + i, 32, stride=16), :] = factor * right[:, half]

    kept.wait()
    for cp in moved:
        cp.wait()
    turn[...] = pbuf[...].astype(F32).reshape(2048, 128)
    _, _, weight, cross = of_group(0, 0)

    @pl.loop(0, 8, unroll=8)
    def _(b, weight=weight, cross=cross):
        at = aligned(b, 256)
        v = jnp.concatenate([turn[pl.ds(2 * b + k, 128, stride=16), :] for k in range(2)], axis=1)
        cur[:, at] = v
        fresh = norm(v, twice(par[0]), twice(par[2])).astype(BF16)
        normed[:, at] = fresh
        project(weight, cross, b, fresh)

    later = []

    def tri_columns(u, b):
        v = jnp.concatenate([turn[pl.ds(2 * b + k, 128, stride=16), :] for k in range(2)], axis=1)
        return norm(v, twice(par[4 + u]), twice(par[6 + u])).astype(BF16)

    def landing(u, k):
        row = spot_row if (u, k) == (0, 0) else r
        return lr.at[u, k, c, aligned(row, 16)]

    def send_lr(u, k, sem, h2, r2, c2):
        pltpu.make_async_remote_copy(
            src_ref=stage.at[u, h2, k], dst_ref=landing(u, k), send_sem=lr_send.at[u], recv_sem=sem,
            device_id=(r2, c2), device_id_type=MESH,
        ).start()

    def arrived(src, dst, send, recv):
        return pltpu.make_async_remote_copy(
            src_ref=src, dst_ref=dst, send_sem=send, recv_sem=recv, device_id=(r, peers[0]), device_id_type=MESH
        )

    for u in range(2):
        first, second = (1, 0) if u == 0 else (0, 1)
        for q in range(4):
            g, rows_g, weight, cross = of_group(u, q)
            if q > 0:

                @pl.loop(0, 8, unroll=8)
                def _(b, weight=weight, cross=cross):
                    project(weight, cross, b, normed[:, aligned(b, 256)])

            for k in range(2):
                stage[u, rows_g, k] = turn_lr[512 * k : 512 * (k + 1), :].astype(BF16).reshape(32, 16, 128)

            each(g, functools.partial(send_lr, u, first, first_recv.at[u]), 1 if q == 0 else 0)

        for q in range(4):
            if u == 0:
                g = lax.rem(group + q, 4)
                each(g, functools.partial(send_lr, u, second, second_recv.at[u, q]), 1 if q == 0 else 0)
            else:
                @pl.loop(1 if q == 0 else 0, 32)
                def _(j, u=u, q=q):
                    r2 = lax.rem(r + j, 32)
                    send_lr(u, second, second_recv.at[u, q], hidden_row(r2) * 4 + turned[q], r2, turned[q])

        for k, sem in ((first, first_recv.at[u]), (second, second_recv.at[u, 0])):
            pltpu.make_async_copy(stage.at[u, mine, k], landing(u, k), sem).start()
        if u == 0:
            for cp in kept_w[2:] + moved_g + moved_w1:
                cp.wait()

        @pl.loop(0, 8, unroll=8)
        def _(b, u=u):
            at = aligned(b, 256)
            gate[:, at] = sigmoid(dot(wgate_all[u], normed[:, at]))

        arrived(lr.at[u, first], lr.at[u, first], lr_send.at[u], first_recv.at[u]).wait_recv()
        later.append(arrived(stage.at[u, pl.ds(0, 127)], stage.at[u, pl.ds(0, 127)], lr_send.at[u], first_recv.at[u]))

        def send_t(sem, _, r2, c2, u=u):
            row = hidden_row(r2) if u == 0 else r2
            pltpu.make_async_remote_copy(
                src_ref=tbuf.at[u, c2, aligned(row, 16)], dst_ref=tri.at[u, mine],
                send_sem=t_send.at[u], recv_sem=sem, device_id=(r2, c2), device_id_type=MESH,
            ).start()

        for q in range(4):
            if u == 0:
                g = lax.rem(group + 4 - q, 4)
                rows_g = aligned(g, 128)
                part = lr.at[0, 0, :, rows_g]
                arrived(part, part, lr_send.at[u], second_recv.at[u, q]).wait_recv()
                left = jnp.concatenate([lr[0, 0, k, rows_g, :] for k in range(4)], axis=1)
                right = jnp.concatenate([lr[0, 1, k] for k in range(4)], axis=1)
                product = dot(left, right, ((1,), (1,))).astype(BF16)
                for k in range(4):
                    tbuf[0, k, rows_g, :] = product[:, 128 * k : 128 * (k + 1)]
                each(g, functools.partial(send_t, t_recv.at[0, q]), 1 if q == 0 else 0)
            else:
                c2 = lax.rem(c + 4 - q, 4)
                part = lr.at[1, 1, c2]
                arrived(part, part, lr_send.at[u], second_recv.at[u, q]).wait_recv()
                left = jnp.concatenate([lr[1, 0, k] for k in range(4)], axis=1)
                tbuf[1, c2] = dot(left, part[...], ((0,), (0,))).astype(BF16)

                @pl.loop(1 if q == 0 else 0, 32)
                def _(j, c2=c2, send_t=send_t):
                    send_t(t_recv.at[1, 0], None, lax.rem(r + j, 32), c2)

        pltpu.make_async_copy(
            tbuf.at[u, c, aligned(spot_row if u == 0 else r, 16)], tri.at[u, mine], t_recv.at[u, 0]
        ).start()
        later.append(
            pltpu.make_async_remote_copy(
                src_ref=tri.at[u, pl.ds(0, 127)], dst_ref=tri.at[u, pl.ds(0, 127)], send_sem=t_send.at[u],
                recv_sem=t_recv.at[u, 0], device_id=(r, peers[0]), device_id_type=MESH,
            )
        )
        if u == 0:
            for q in range(4):
                g = lax.rem(group + q, 4)
                rows_g = tri.at[0, aligned(g, 32)]
                arrived(rows_g, rows_g, t_send.at[0], t_recv.at[0, q]).wait_recv()
                turn[aligned(g, 512), :] = rows_g[...].astype(F32).reshape(512, 128)
        else:
            arrived(tri.at[1], tri.at[1], t_send.at[1], t_recv.at[1, 0]).wait_recv()
            turn[...] = tri[1].astype(F32).reshape(2048, 128)

        if u == 0:
            _, _, weight, cross = of_group(1, 0)

            @pl.loop(0, 8, unroll=8)
            def _(b, weight=weight, cross=cross):
                at = aligned(b, 256)
                update = dot(wout_t[0], tri_columns(0, b))
                new = (cur[:, at] + gate[:, at] * update).astype(BF16).astype(F32)
                cur[:, at] = new
                fresh = norm(new, twice(par[1]), twice(par[3])).astype(BF16)
                normed[:, at] = fresh
                project(weight, cross, b, fresh)

    here = out.at[:, :, aligned(c, 128)]
    last = []
    for turned_half in range(2):
        half = lax.rem(lax.div(c, 2) + 1 + turned_half, 2)
        rows_h = aligned(half, 64)

        @pl.loop(0, 8, unroll=8)
        def _(b, first_half=turned_half == 0, half=half, rows_h=rows_h):
            at = aligned(b, 256)
            if first_half:
                normed[:, at] = tri_columns(1, b)
            update = dot(wout_t[1, rows_h, :], normed[:, at])
            new = cur[rows_h, at] + gate[rows_h, at] * update
            for k in range(2):
                turn_out[pl.ds(2 * b + k, 64, stride=16), :] = new[:, 128 * k : 128 * (k + 1)]

        obuf[rows_h] = turn_out[...].astype(BF16).reshape(64, 16, 128)
        for s in range(2) if turned_half == 0 else (2,):
            c2 = c_peers[s][1]
            cp = pltpu.make_async_remote_copy(
                src_ref=obuf.at[aligned(c2, 32)], dst_ref=here, send_sem=o_send.at[0, s], recv_sem=o_recv.at[0, s],
                device_id=c_peers[s], device_id_type=MESH,
            )
            cp.start()
            last.append(cp)
    own(0, obuf.at[rows_c], here, o_own).wait()
    for cp in last:
        cp.wait()
    for cp in later:
        cp.wait_send()


def per_device(
    pair, residue_mask, chain_ids, pair_gain, pair_bias, in_weight, gate_weight,
    hidden_gain, hidden_bias, cross_gain, out_weight,
):
    dma = pltpu.SemaphoreType.DMA
    return pl.pallas_call(
        kernel,
        out_shape=jax.ShapeDtypeStruct((32, 16, 512), BF16),
        in_specs=[ANY] * 11,
        out_specs=ANY,
        scratch_shapes=[
            pltpu.VMEM((2, 128, 128), BF16),
            pltpu.VMEM((2, 128), F32),
            pltpu.VMEM((2, 128), F32),
            pltpu.VMEM((2, 32), F32),
            pltpu.VMEM((2, 32), F32),
            pltpu.VMEM((2, 32), F32),
            pltpu.VMEM((4, 128), jnp.int32),
            pltpu.VMEM((4, 128), jnp.int32),
            pltpu.VMEM((128, 16, 128), BF16),
            pltpu.VMEM((2, 4, 128, 128), BF16),
            pltpu.VMEM((2, 128, 128), BF16),
            pltpu.VMEM((2, 128, 128), BF16),
            pltpu.VMEM((8, 128), F32),
            pltpu.VMEM((4, 8, 128), F32),
            pltpu.VMEM((10, 128, 128), F32),
            pltpu.VMEM((2, 16, 128), F32),
            pltpu.VMEM((2048, 128), F32),
            pltpu.VMEM((1024, 128), F32),
            pltpu.VMEM((1024, 128), F32),
            pltpu.VMEM((128, 2048), F32),
            pltpu.VMEM((128, 2048), BF16),
            pltpu.VMEM((128, 2048), F32),
            pltpu.VMEM((2, 128, 2, 16, 128), BF16),
            pltpu.VMEM((2, 2, 4, 512, 128), BF16),
            pltpu.VMEM((2, 4, 512, 128), BF16),
            pltpu.VMEM((2, 128, 16, 128), BF16),
            pltpu.VMEM((128, 16, 128), BF16),
            dma((1, 3)), dma((1, 3)), dma((1,)),
            dma((4, 3)), dma((4, 3)), dma((4,)),
            dma((2,)), dma((2,)), dma((2, 4)), dma((2,)), dma((2, 4)),
            dma((1, 3)), dma((1, 3)), dma((1,)), dma((8,)),
            pltpu.SemaphoreType.REGULAR((3,)),
        ],
        compiler_params=pltpu.CompilerParams(
            collective_id=0, has_side_effects=True, vmem_limit_bytes=62 * 2**20
        ),
    )(
        pair,
        jnp.swapaxes(in_weight, 2, 3),
        jnp.swapaxes(gate_weight, 1, 2),
        out_weight,
        pair_gain, pair_bias, hidden_gain, hidden_bias, cross_gain,
        residue_mask.reshape(4, 128), chain_ids.reshape(4, 128),
    )


def solution(mesh):
    placed = (
        P("ch", "rows", None), P(), P(), P(), P(), P(None, None, None, "ch"), P(None, None, "ch"),
        P(None, "ch"), P(None, "ch"), P(None, "ch"), P(),
    )
    return jax.shard_map(
        per_device, mesh=mesh, in_specs=placed, out_specs=P("ch", "rows", None), check_vma=False
    )
```
